32 devices in a mesh: ctx: 16 (over z, y, x), head: 2 (over core).
Axes of the slice: x: 2, y: 2, z: 4, core: 2. Of those that a mesh axis runs over, the one named last changes fastest.
Arguments:
- inputs: bfloat16 [2048, 2048], P('ctx', 'head'), may hold values from -6 to 6
- queries: bfloat16 [2048, 32, 128], P('ctx', 'head'), may hold values from -6 to 6
- keys: bfloat16 [2048, 4, 128], P('ctx', 'head'), may hold values from -6 to 6
- values: bfloat16 [2048, 4, 128], P('ctx', 'head'), may hold values from -6 to 6
- lengths: int32 [4], replicated, may hold values from 1 to 1024, 2048 in all
- out_weight: bfloat16 [4096, 2048], P('head'), may hold values from -0.09375 to 0.09375
- norm_gain: bfloat16 [2048], P('head'), may hold values from 0.099609375 to 1.8984375
- expert_ids: int32 [2048, 8], P('ctx'), may hold values from 0 to 31, all different within a row; in each aligned block of 128 rows (0 to 127, 128 to 255, ...) at most 40 rows name the same one
- gate_codes: int32 [2048, 8], P('ctx'), may hold values from 1 to 16
- gate_weight: bfloat16 [32, 2048, 768], P('ctx', None, 'head'), may hold values from -0.125 to 0.125
- up_weight: bfloat16 [32, 2048, 768], P('ctx', None, 'head'), may hold values from -0.125 to 0.125
- down_weight: bfloat16 [32, 768, 2048], P('ctx', 'head'), may hold values from -0.4375 to 0.4375
- cotangent: bfloat16 [2048, 2048], P('ctx', 'head'), may hold values from -6 to 6
Outputs:
- output: bfloat16 [2048, 2048], P('ctx', 'head')
- input_grad: bfloat16 [2048, 2048], P('ctx', 'head')
- down_grad: bfloat16 [32, 768, 2048], P('ctx', 'head')
- norm_term: float32 [2048], P('ctx')
The draws below stay inside these ranges and needn't reach their ends.
Inputs may be any that keep to these rules, and one draw needn't show every extreme that they name: `expert_ids`: the 128 rows of one index of ctx name one expert at most 40 times, a bound that some block reaches. The lengths sum to 2048; the largest is 1024.
All inputs are finite; a program needn't handle non-finite values.
Results may differ from the reference program's by a relative error of at most 0.023.
Values may be sent and summed in bfloat16 or wider, within the bound.
No kernel may reach another device: no remote copies, remote signals or barrier semaphores. Data moves between devices by JAX's collectives and lax.ppermute only.
A program may use at most 256 MiB of HBM per device.

```python
import math
import jax
import jax.numpy as jnp
import numpy as np
from jax import lax

D = 2048
QUERY_HEADS = 32
KEY_VALUE_HEADS = 4
HEAD_SIZE = 128
FF = 768
TOP = 8
TOK_DEV = 128
EXPERTS = 32
PACKED_TOKENS = 2048
CAP = 40
MAXDOC = 1024
DOCS = 4
N_CTX = 16


def draw_queries(key, part):
    final_result = jnp.clip(jax.random.normal(jax.random.fold_in(key, 1), (PACKED_TOKENS, QUERY_HEADS, HEAD_SIZE), jnp.float32), -6.0, 6.0)
    return final_result.astype(jnp.bfloat16)


def draw_keys(key, part):
    final_result = jnp.clip(jax.random.normal(jax.random.fold_in(key, 2), (PACKED_TOKENS, KEY_VALUE_HEADS, HEAD_SIZE), jnp.float32), -6.0, 6.0)
    return final_result.astype(jnp.bfloat16)


def set_ends(array, rng, low, largest):
    longest = array.shape.index(max(array.shape))
    spots = []
    for shift in (0, 1):
        where = [jax.random.randint(jax.random.fold_in(rng, axis), (), 0, length) for axis, length in enumerate(array.shape)]
        where[longest] = (where[longest] + shift) % array.shape[longest]
        spots.append(tuple(where))
    return array.at[spots[0]].set(low).at[spots[1]].set(largest)


def level_of(own_key, shape, split, least, high):
    loudness, own = 1.0, jax.random.fold_in(own_key, 6)
    for dim, parts in split:
        heights = jnp.exp(jax.random.uniform(jax.random.fold_in(own, dim), (parts,), jnp.float32, least / len(split), high / len(split)))
        loudness = loudness * jnp.repeat(heights, shape[dim] // parts).reshape([-1 if axis == dim else 1 for axis in range(len(shape))])
    return loudness


def length_profile(number_of, total, limit, slope):
    portions = [(1 << 20) // math.isqrt(rank ** slope) + 1 for rank in range(2, number_of + 1)]
    rest, holding = total - limit - (number_of - 1), [1] * (number_of - 1)
    while rest > 0:
        free = [i for i in range(number_of - 1) if holding[i] < limit]
        mass, left = sum([portions[i] for i in free]), rest
        for i in free:
            extra = min(limit - holding[i], max(1, left * portions[i] // mass), rest)
            holding[i] = holding[i] + extra
            rest = rest - extra
    return np.array([limit] + holding)


def ragged(rng, amount, total, limit, skew):
    if amount == 2:
        one = jax.random.randint(rng, (), max(1, total - limit), min(limit, total - 1) + 1)
        return jnp.stack([one, total - one])
    tallies = jnp.asarray(length_profile(amount, total, limit, skew), jnp.int32)
    pairs = (amount - 1) // 2
    giver, receiver = tallies[1:1 + 2 * pairs:2], tallies[2:2 + 2 * pairs:2]
    slack = jnp.minimum(giver - 1, limit - receiver)
    moved = jax.random.randint(jax.random.fold_in(rng, 1), (pairs,), 0, 1 << 20) % (slack + 1)
    tallies = tallies.at[1:1 + 2 * pairs:2].set(giver - moved).at[2:2 + 2 * pairs:2].set(receiver + moved)
    return tallies[jax.random.permutation(jax.random.fold_in(rng, 2), amount)]


def deal_out(rng, own, number, rows, count, top, most, slope):
    sequence = jax.random.permutation(rng, count)
    crowded, usual = load_shares(count, rows * top, most, slope, True), load_shares(count, rows * top, most, slope, False)
    places = jnp.arange(count)

    def named(sizes, rotation):
        used = int((sizes > 0).sum())
        fixed = max(1, used // 4)
        passed = fixed + (places - fixed + rotation * (used - fixed)) % max(1, count - fixed)
        return jnp.zeros((count,), jnp.int32).at[sequence[jnp.where(places < fixed, places, passed)]].set(jnp.asarray(sizes, jnp.int32))

    sizes = jnp.where(number % 4 == 0, named(crowded, number // 4), named(usual, number - number // 4 - 1))
    mixed = jax.random.permutation(jax.random.fold_in(own, 3), count)
    giver, receiver = mixed[0:count // 2 * 2:2], mixed[1:count // 2 * 2:2]
    slack = jnp.minimum(sizes[giver] - 1, most - sizes[receiver]) // 2
    slack = jnp.where((giver == sequence[0]) | (receiver == sequence[0]) | (sizes[receiver] == 0), 0, jnp.maximum(slack, 0))
    passed = jax.random.randint(jax.random.fold_in(own, 4), (count // 2,), 0, 1 << 20) % (slack + 1)
    sizes = sizes.at[giver].add(-passed).at[receiver].add(passed)
    members = jnp.searchsorted(jnp.cumsum(sizes), jnp.arange(rows * top), side="right").astype(jnp.int32)
    table = members.reshape(top, rows).T
    table = table[jax.random.permutation(jax.random.fold_in(own, 1), rows)]
    rotation = jax.random.randint(jax.random.fold_in(own, 2), (rows, 1), 0, top)
    return jnp.take_along_axis(table, (jnp.arange(top)[None, :] + rotation) % top, axis=1)


def load_shares(amount, total, most, slope, full):
    loads = [(1 << 20) // math.isqrt(rank ** slope) + 1 for rank in range(1, amount + 1)]
    largest = most if full else min(most, max(-(-total // amount), total * loads[0] // sum(loads)))
    least = 1 if total - largest >= amount - 1 else 0
    counts, surplus = [largest] + [least] * (amount - 1), total - largest - least * (amount - 1)
    while surplus > 0:
        movable = [i for i in range(1, amount) if counts[i] < largest] or [i for i in range(1, amount) if counts[i] < most]
        whole, budget = sum([loads[i] for i in movable]), surplus
        for i in movable:
            more = min(most - counts[i], max(1, budget * loads[i] // whole), surplus)
            counts[i] = counts[i] + more
            surplus = surplus - more
    return np.array(counts)


def gaussian(rng, extent, spread, bound, shards=(), kind=jnp.bfloat16):
    loudness = level_of(rng, extent, shards, -0.22, 0.18) if shards else 1.0
    drawn = jax.random.normal(rng, extent, jnp.float32) * spread * loudness
    return jnp.minimum(jnp.maximum(drawn, -bound), bound).astype(kind)


def setup_inputs(seed: int = 0) -> dict:
    key_of = jax.random.split(jax.random.key(seed), 14)
    inputs = gaussian(key_of[0], (PACKED_TOKENS, D), 1.0, 6.0, ((0, 16), (1, 2)))
    queries = draw_queries(jax.random.fold_in(key_of[13], 71), 0)
    keys = draw_keys(jax.random.fold_in(key_of[13], 71), 0)
    values = gaussian(key_of[3], (PACKED_TOKENS, KEY_VALUE_HEADS, HEAD_SIZE), 1.0, 6.0, ((0, 16), (1, 2)))
    lengths = ragged(key_of[4], DOCS, PACKED_TOKENS, MAXDOC, 2).astype(jnp.int32)
    out_weight = gaussian(key_of[5], (QUERY_HEADS * HEAD_SIZE, D), (QUERY_HEADS * HEAD_SIZE) ** -0.5, 0.09375, ((0, 2),))
    norm_gain = jnp.clip(1.0 + 0.18 * jax.random.normal(key_of[6], (D,), jnp.float32), 0.099609375, 1.8984375).astype(jnp.bfloat16)
    expert_ids_keys = jax.random.split(jax.random.fold_in(key_of[7], 1), PACKED_TOKENS // TOK_DEV)
    expert_ids_turns = jax.random.permutation(jax.random.fold_in(key_of[7], 3), PACKED_TOKENS // TOK_DEV)
    expert_ids = jax.vmap(lambda own, number: deal_out(jax.random.fold_in(key_of[7], 2), own, number, TOK_DEV, EXPERTS, TOP, CAP, 2))(expert_ids_keys, expert_ids_turns).reshape((PACKED_TOKENS, TOP))
    gate_codes = set_ends(jax.random.randint(key_of[8], (PACKED_TOKENS, TOP), 1, 17), jax.random.fold_in(key_of[8], 1), 1, 16).astype(jnp.int32)
    gate_weight = gaussian(key_of[9], (EXPERTS, D, FF), D ** -0.5, 0.125, ((0, 16), (2, 2)))
    up_weight = gaussian(key_of[10], (EXPERTS, D, FF), D ** -0.5, 0.125, ((0, 16), (2, 2)))
    down_weight = gaussian(key_of[11], (EXPERTS, FF, D), (FF // 4) ** -0.5, 0.4375, ((0, 16), (1, 2)))
    cotangent = gaussian(key_of[12], (PACKED_TOKENS, D), 1.0, 6.0, ((0, 16), (1, 2)))
    return dict(inputs=inputs, queries=queries, keys=keys, values=values, lengths=lengths, out_weight=out_weight, norm_gain=norm_gain, expert_ids=expert_ids, gate_codes=gate_codes, gate_weight=gate_weight, up_weight=up_weight, down_weight=down_weight, cotangent=cotangent)


def rows_by_position():
    places = jnp.arange(PACKED_TOKENS, dtype=jnp.int32)
    half = TOK_DEV // 2
    blocknum = places // half
    inside = places % half
    owner = jnp.where(blocknum < N_CTX, blocknum, 2 * N_CTX - 1 - blocknum)
    within = jnp.where(blocknum < N_CTX, inside, half + inside)
    return (owner * TOK_DEV + within).astype(jnp.int32)

def document_ids(places, lengths):
    ends = jnp.cumsum(lengths).astype(jnp.int32)
    return lax.optimization_barrier(jnp.sum((places[:, None] >= ends[None, :]).astype(jnp.int32), axis=1)).astype(jnp.int32)

def attention(queries, keys, values, lengths):
    ordering = rows_by_position()
    query_sorted = queries[ordering]
    key_sorted = keys[ordering]
    value_sorted = values[ordering]
    documents = document_ids(jnp.arange(PACKED_TOKENS, dtype=jnp.int32), lengths)
    block_of_query = min(512, PACKED_TOKENS)
    key_width = min(PACKED_TOKENS, MAXDOC + block_of_query)
    head_groups = QUERY_HEADS // KEY_VALUE_HEADS
    scale = HEAD_SIZE ** (-0.5)

    def one_block(index):
        query_start = (index * block_of_query).astype(jnp.int32)
        key_start = jnp.maximum(query_start + block_of_query - key_width, 0).astype(jnp.int32)
        query_portion = lax.dynamic_slice_in_dim(query_sorted, query_start, block_of_query, 0).astype(jnp.float32)
        query_portion = query_portion.reshape(block_of_query, KEY_VALUE_HEADS, head_groups, HEAD_SIZE)
        key_part = lax.dynamic_slice_in_dim(key_sorted, key_start, key_width, 0).astype(jnp.float32)
        value_part = lax.dynamic_slice_in_dim(value_sorted, key_start, key_width, 0).astype(jnp.float32)
        scores = jnp.einsum('qkgd,skd->kgqs', query_portion, key_part) * scale
        query_places = query_start + jnp.arange(block_of_query, dtype=jnp.int32)
        key_places = key_start + jnp.arange(key_width, dtype=jnp.int32)
        query_docs = lax.dynamic_slice_in_dim(documents, query_start, block_of_query, 0)
        key_docs = lax.dynamic_slice_in_dim(documents, key_start, key_width, 0)
        allowed = (key_places[None, :] <= query_places[:, None]) & (key_docs[None, :] == query_docs[:, None])
        masked = jnp.where(allowed, scores, -1e+30)
        highest = lax.optimization_barrier(jnp.max(masked, axis=-1, keepdims=True))
        weights = jnp.where(allowed, jnp.exp(scores - highest), 0.0)
        denominator = lax.optimization_barrier(jnp.sum(weights, axis=-1))
        rounded = lax.optimization_barrier(weights.astype(jnp.bfloat16)).astype(jnp.float32)
        mixed = jnp.einsum('kgqs,skd->qkgd', rounded, value_part)
        mixed = mixed / jnp.transpose(denominator, (2, 0, 1))[..., None]
        return mixed.reshape(block_of_query, QUERY_HEADS * HEAD_SIZE).astype(jnp.bfloat16)
    blocks = lax.map(one_block, jnp.arange(PACKED_TOKENS // block_of_query, dtype=jnp.int32))
    in_position = blocks.reshape(PACKED_TOKENS, QUERY_HEADS * HEAD_SIZE)
    return jnp.zeros_like(in_position).at[ordering].set(in_position)

def slot_numbers(expert_ids):
    flat = expert_ids.reshape(N_CTX, TOK_DEV * TOP)
    onehot = (flat[:, :, None] == jnp.arange(EXPERTS, dtype=jnp.int32)[None, None, :]).astype(jnp.int32)
    ranks = (jnp.cumsum(onehot, axis=1) - 1).astype(jnp.int32)
    return lax.optimization_barrier(jnp.sum(ranks * onehot, axis=2)).astype(jnp.int32).reshape(PACKED_TOKENS * TOP)

def reference(inputs, queries, keys, values, lengths, out_weight, norm_gain, expert_ids, gate_codes, gate_weight, up_weight, down_weight, cotangent):
    heads = attention(queries, keys, values, lengths)
    stream = (inputs.astype(jnp.float32) + jnp.dot(heads, out_weight, preferred_element_type=jnp.float32)).astype(jnp.bfloat16)
    wide = stream.astype(jnp.float32)
    inverse = lax.rsqrt(lax.optimization_barrier(jnp.mean(wide * wide, axis=1, keepdims=True)) + 1e-06)
    gain = norm_gain.astype(jnp.float32)
    normed = (wide * inverse * gain).astype(jnp.bfloat16)
    shares = gate_codes.astype(jnp.float32)
    shares = shares / lax.optimization_barrier(jnp.sum(shares, axis=1, keepdims=True))
    flat_experts = expert_ids.reshape(PACKED_TOKENS * TOP).astype(jnp.int32)
    slots = slot_numbers(expert_ids)
    sources = (jnp.arange(PACKED_TOKENS * TOP, dtype=jnp.int32) // TOP).astype(jnp.int32)
    columns = (sources // TOK_DEV * CAP + slots).astype(jnp.int32)
    depth = N_CTX * CAP
    routed = jnp.zeros((EXPERTS, depth, D), jnp.bfloat16).at[flat_experts, columns].set(normed[sources])

    def forward_expert(packed):
        rows, gate_w, up_w, down_w = packed
        gate = jnp.dot(rows, gate_w, preferred_element_type=jnp.float32)
        upper = jnp.dot(rows, up_w, preferred_element_type=jnp.float32)
        units = (jax.nn.silu(gate) * upper).astype(jnp.bfloat16)
        return jnp.dot(units, down_w, preferred_element_type=jnp.float32).astype(jnp.bfloat16)
    expert_out = lax.map(forward_expert, (routed, gate_weight, up_weight, down_weight))
    picked = expert_out[flat_experts, columns].astype(jnp.float32).reshape(PACKED_TOKENS, TOP, D)
    mixture = lax.optimization_barrier(jnp.sum(picked * shares[:, :, None], axis=1))
    output = (wide + mixture).astype(jnp.bfloat16)
    upstream = cotangent.astype(jnp.float32)
    routed_rows = (shares[:, :, None] * upstream[:, None, :]).astype(jnp.bfloat16).reshape(PACKED_TOKENS * TOP, D)
    routed_grad = jnp.zeros((EXPERTS, depth, D), jnp.bfloat16).at[flat_experts, columns].set(routed_rows)

    def backward_expert(packed):
        rows, incoming, gate_w, up_w, down_w = packed
        gate = jnp.dot(rows, gate_w, preferred_element_type=jnp.float32)
        upper = jnp.dot(rows, up_w, preferred_element_type=jnp.float32)
        activated = jax.nn.silu(gate)
        units = (activated * upper).astype(jnp.bfloat16)
        units_grad = jnp.dot(incoming, down_w.T, preferred_element_type=jnp.float32)
        sigmoid_gate = jax.nn.sigmoid(gate)
        gate_grad = (units_grad * upper * sigmoid_gate * (1.0 + gate * (1.0 - sigmoid_gate))).astype(jnp.bfloat16)
        up_grad = (units_grad * activated).astype(jnp.bfloat16)
        down_part = jnp.dot(units.T, incoming, preferred_element_type=jnp.float32).astype(jnp.bfloat16)
        back = (jnp.dot(gate_grad, gate_w.T, preferred_element_type=jnp.float32) + jnp.dot(up_grad, up_w.T, preferred_element_type=jnp.float32)).astype(jnp.bfloat16)
        return (down_part, back)
    down_grad, back = lax.map(backward_expert, (routed, routed_grad, gate_weight, up_weight, down_weight))
    gathered = back[flat_experts, columns].astype(jnp.float32).reshape(PACKED_TOKENS, TOP, D)
    scaled = lax.optimization_barrier(jnp.sum(gathered, axis=1)) * gain
    inner = lax.optimization_barrier(jnp.sum(scaled * wide, axis=1, keepdims=True))
    input_grad = (upstream + inverse * scaled - wide * inverse ** 3 * inner / D).astype(jnp.bfloat16)
    norm_term = (inverse ** 2 * inner / D ** 0.5)[:, 0]
    return (output, input_grad, down_grad, norm_term)
```

```python
import jax
import jax.numpy as jnp
from jax import lax
from jax.sharding import PartitionSpec as P

D = 2048
TOP = 8
EXP_DEV = 2
TOK_DEV = 128
BF = jnp.bfloat16
F32 = jnp.float32
AXES = ("ctx", "head")


def grid_of(devices):
    side = 2 if devices < 64 else 4
    return devices // (side * side), side


def exchange(array, devices, masks):
    pairs = [
        (c * 2 + h, (c ^ masks[h]) * 2 + h) for c in range(devices) for h in range(2)
    ]
    return lax.ppermute(array, AXES, pairs)


def swap_cores(array, devices):
    pairs = [(c * 2 + h, c * 2 + 1 - h) for c in range(devices) for h in range(2)]
    return lax.ppermute(array, AXES, pairs)


def local(
    inputs,
    queries,
    keys,
    values,
    lengths,
    out_weight,
    norm_gain,
    expert_ids,
    gate_codes,
    gate_weight,
    up_weight,
    down_weight,
    cotangent,
):
    devices = lax.axis_size("ctx")
    position = lax.axis_index("ctx")
    head = lax.axis_index("head")
    deep, side = grid_of(devices)
    plane = side * side

    def z_masks(k):
        return (k * plane, k * plane)

    def a_masks(k):
        return (k, k * side)

    def b_masks(k):
        return (k * side, k)

    def along(array, masks_of, count):
        return [array] + [exchange(array, devices, masks_of(k)) for k in range(1, count)]

    local_tokens, local_heads, head_width = queries.shape
    kv_heads = keys.shape[1]
    head_groups = local_heads // kv_heads
    half_width = inputs.shape[1]
    capacity = max(2, 5 * TOK_DEV * TOP // (4 * EXP_DEV * devices))
    block_rows = -(-deep * capacity // 16) * 16

    packed = jnp.concatenate(
        [
            keys.transpose(1, 0, 2).reshape(kv_heads * local_tokens, head_width),
            values.transpose(1, 0, 2).reshape(kv_heads * local_tokens, head_width),
            expert_ids.T.astype(BF),
            gate_codes.T.astype(BF),
        ],
        axis=0,
    )
    pack_z = jnp.stack(along(packed, z_masks, deep))
    pack_a = jnp.stack(along(pack_z, a_masks, side))
    pack_b = jnp.stack(along(pack_a, b_masks, side))
    chunks = devices
    pack_all = pack_b.reshape(chunks, packed.shape[0], head_width)
    key_piece = pack_all[:, : kv_heads * local_tokens].reshape(
        chunks, kv_heads, local_tokens, head_width
    )
    value_piece = pack_all[:, kv_heads * local_tokens : 2 * kv_heads * local_tokens].reshape(
        chunks, kv_heads, local_tokens, head_width
    )

    order = jnp.arange(chunks, dtype=jnp.int32)
    z_part, a_part, b_part = order % deep, order // deep % side, order // (deep * side)
    shift = jnp.where(head == 0, a_part + b_part * side, a_part * side + b_part)
    sources = position ^ (z_part * plane + shift)

    def places_of(owner):
        within = jnp.arange(local_tokens, dtype=jnp.int32)
        half = local_tokens // 2
        owner = owner[..., None]
        return jnp.where(
            within < half, owner * half + within, (2 * devices - 1 - owner) * half + within - half
        )

    docs_in = lengths.shape[0]
    upto = jnp.arange(docs_in)[:, None] <= jnp.arange(docs_in)[None, :]
    ends = jnp.sum(jnp.where(upto, lengths[:, None], 0), axis=0)

    def docs_of(places):
        return jnp.sum((places[..., None] >= ends).astype(jnp.int32), axis=-1)

    query_places = places_of(position[None])[0]
    query_docs = docs_of(query_places)
    key_places = places_of(sources)
    key_docs = docs_of(key_places)
    allowed = (key_places[None] <= query_places[:, None, None]) & (
        key_docs[None] == query_docs[:, None, None]
    )
    scale = head_width ** (-0.5)
    grouped = queries.reshape(local_tokens, kv_heads, head_groups, head_width).transpose(1, 2, 0, 3)
    scores = jnp.einsum("kgqd,cksd->kgqcs".replace(" ", ""), grouped, key_piece, preferred_element_type=F32)
    scores = scores * scale
    masked = jnp.where(allowed, scores, -1e30)
    top = jnp.max(masked, axis=(3, 4), keepdims=True)
    weights = jnp.where(allowed, jnp.exp(scores - top), 0.0)
    denominator = jnp.sum(weights, axis=(3, 4))
    mixed = jnp.einsum("kgqcs,cksd->kgqd", weights.astype(BF), value_piece, preferred_element_type=F32)
    heads = (mixed / denominator[..., None]).astype(BF)
    heads = heads.transpose(2, 0, 1, 3).reshape(local_tokens, local_heads * head_width)

    partial_proj = jnp.dot(heads, out_weight, preferred_element_type=F32)
    mine = lax.dynamic_slice_in_dim(partial_proj, head * half_width, half_width, 1)
    theirs = lax.dynamic_slice_in_dim(partial_proj, (1 - head) * half_width, half_width, 1)
    projected = mine + swap_cores(theirs.astype(BF), devices).astype(F32)
    stream = (inputs.astype(F32) + projected).astype(BF)
    wide = stream.astype(F32)
    squares = lax.psum(jnp.sum(wide * wide, axis=1), "head")
    inverse = lax.rsqrt(squares / D + 1e-06)[:, None]
    gain = norm_gain.astype(F32)
    normed = (wide * inverse * gain).astype(BF)

    near = pack_a[..., -2 * TOP :, :].astype(jnp.int32)
    near_ids, near_codes = near[..., :TOP, :], near[..., TOP:, :].astype(F32)
    near_total = jnp.sum(near_codes, axis=-2)
    owners = position ^ (jnp.arange(side, dtype=jnp.int32) * jnp.where(head == 0, side, 1))
    experts = owners[:, None] * EXP_DEV + jnp.arange(EXP_DEV, dtype=jnp.int32)
    hit = near_ids == experts[:, :, None, None, None, None]
    share = jnp.sum(jnp.where(hit, near_codes, 0.0), axis=-2) / near_total
    member = jnp.any(hit, axis=-2)
    before = jnp.arange(local_tokens)[:, None] < jnp.arange(local_tokens)[None, :]
    rank = jnp.einsum(
        "keazt,tu->keazu", member.astype(BF), before.astype(BF), preferred_element_type=F32
    ).astype(jnp.int32)
    slot = jnp.arange(deep, dtype=jnp.int32)[:, None] * capacity + rank
    slot = jnp.where(member, slot, -1)
    tokens = deep * local_tokens
    slot = slot.reshape(side, EXP_DEV, side, tokens)
    share = share.reshape(side, EXP_DEV, side, tokens)
    hot = slot[..., None, :] == jnp.arange(block_rows, dtype=jnp.int32)[:, None]
    hot_bf = hot.astype(BF)
    slot_share = jnp.sum(jnp.where(hot, share[..., None, :], 0.0), axis=-1)

    def send_rows(rows, scaled):
        level = jnp.stack(along(rows, z_masks, deep))
        level = jnp.stack(along(level, a_masks, side)).reshape(side, tokens, half_width)
        out = jnp.einsum("kearu,aud->keard", hot_bf, level, preferred_element_type=F32)
        if scaled:
            out = out * slot_share[..., None]
        out = out.astype(BF)
        got = [out[0]] + [exchange(out[k], devices, b_masks(k)) for k in range(1, side)]
        got = jnp.stack(got)
        other = swap_cores(got, devices).transpose(2, 1, 0, 3, 4)
        return jnp.where(
            head == 0,
            jnp.concatenate([got, other], axis=-1),
            jnp.concatenate([other, got], axis=-1),
        )

    def return_rows(part, weighted):
        mine = lax.dynamic_slice_in_dim(part, head * half_width, half_width, 4)
        theirs = lax.dynamic_slice_in_dim(part, (1 - head) * half_width, half_width, 4)
        theirs = theirs.astype(BF).transpose(2, 1, 0, 3, 4)
        total = (mine + swap_cores(theirs, devices).astype(F32)).astype(BF)
        got = [total[0]] + [exchange(total[k], devices, b_masks(k)) for k in range(1, side)]
        got = jnp.stack(got)
        if weighted:
            each = jnp.einsum("kearu,keard->keaud", hot_bf, got, preferred_element_type=F32)
            dense = jnp.sum(each * share[..., None], axis=(0, 1))
        else:
            dense = jnp.einsum("kearu,keard->aud", hot_bf, got, preferred_element_type=F32)
        near_sum = dense[0]
        for k in range(1, side):
            near_sum = near_sum + exchange(dense[k].astype(BF), devices, a_masks(k)).astype(F32)
        near_sum = near_sum.reshape(deep, local_tokens, half_width)
        result = near_sum[0]
        for k in range(1, deep):
            result = result + exchange(near_sum[k].astype(BF), devices, z_masks(k)).astype(F32)
        return result

    upstream = cotangent.astype(F32)
    incoming = send_rows(cotangent, True)
    features = send_rows(normed, False)
    gate = jnp.einsum("beard,edf->bearf", features, gate_weight, preferred_element_type=F32)
    upper = jnp.einsum("beard,edf->bearf", features, up_weight, preferred_element_type=F32)
    sigmoid_gate = jax.nn.sigmoid(gate)
    activated = gate * sigmoid_gate
    units = (activated * upper).astype(BF)
    partial_out = jnp.einsum("bearf,efd->beard", units, down_weight, preferred_element_type=F32)
    mixture = return_rows(partial_out, True)
    output = (wide + mixture).astype(BF)

    units_grad = jnp.einsum("beard,efd->bearf", incoming, down_weight, preferred_element_type=F32)
    gate_grad = (units_grad * upper * sigmoid_gate * (1.0 + gate * (1.0 - sigmoid_gate))).astype(BF)
    up_grad = (units_grad * activated).astype(BF)
    down_grad = jnp.einsum(
        "bearf,beard->efd", units, incoming, preferred_element_type=F32
    ).astype(BF)
    input_part = jnp.einsum(
        "bearf,edf->beard", gate_grad, gate_weight, preferred_element_type=F32
    ) + jnp.einsum("bearf,edf->beard", up_grad, up_weight, preferred_element_type=F32)
    scaled = return_rows(input_part, False) * gain
    inner = lax.psum(jnp.sum(scaled * wide, axis=1), "head")[:, None]
    input_grad = (upstream + inverse * scaled - wide * inverse**3 * inner / D).astype(BF)
    norm_term = (inverse**2 * inner / D**0.5)[:, 0]
    return (output, input_grad, down_grad, norm_term)


def solution(mesh):
    in_specs = (
        P("ctx", "head"),
        P("ctx", "head", None),
        P("ctx", "head", None),
        P("ctx", "head", None),
        P(),
        P("head", None),
        P("head"),
        P("ctx", None),
        P("ctx", None),
        P("ctx", None, "head"),
        P("ctx", None, "head"),
        P("ctx", "head", None),
        P("ctx", "head"),
    )
    out_specs = (P("ctx", "head"), P("ctx", "head"), P("ctx", "head", None), P("ctx"))
    return jax.shard_map(local, mesh=mesh, in_specs=in_specs, out_specs=out_specs, check_vma=False)
```

```python
import jax
import jax.numpy as jnp
from jax import lax
from jax.experimental import pallas as pl
from jax.experimental.pallas import tpu as pltpu
from jax.sharding import PartitionSpec as P

D = 2048
TOP = 8
EXP_DEV = 2
TOK_DEV = 128
BF = jnp.bfloat16
F32 = jnp.float32
AXES = ("ctx", "head")
CHEAP = pl.CostEstimate(flops=1, bytes_accessed=1, transcendentals=0)


def grid_of(devices):
    side = 2 if devices < 64 else 4
    return devices // (side * side), side


def exchange(array, devices, masks):
    pairs = [
        (c * 2 + h, (c ^ masks[h]) * 2 + h) for c in range(devices) for h in range(2)
    ]
    return lax.ppermute(array, AXES, pairs)


def swap_cores(array, devices):
    pairs = [(c * 2 + h, c * 2 + 1 - h) for c in range(devices) for h in range(2)]
    return lax.ppermute(array, AXES, pairs)


def after(value, *others):
    return lax.optimization_barrier((value, others))[0]


def attend_kernel(first, last, head_groups, q_ref, kv_ref, place_ref, low_ref, high_ref, *refs):
    refs = list(refs)
    carry = None if first else [refs.pop(0) for _ in range(3)]
    outs = [refs.pop(0) for _ in range(1 if last else 3)]
    bias_ref = refs[0]
    heads, tokens, width = q_ref.shape
    chunks = kv_ref.shape[0]
    count = chunks * tokens
    kv_heads = heads // head_groups
    place = place_ref[...]
    seen = (place >= low_ref[...]) & (place <= high_ref[...])
    bias_ref[...] = jnp.where(seen, 0.0, -1e30)
    factor = width ** (-0.5) * 1.4426950408889634
    for kv in range(kv_heads):
        key = kv_ref[:, kv * tokens : (kv + 1) * tokens, :].reshape(count, width)
        start = (kv_heads + kv) * tokens
        value = kv_ref[:, start : start + tokens, :].reshape(count, width)
        for group in range(head_groups):
            head = kv * head_groups + group
            scores = lax.dot_general(
                q_ref[head], key, (((1,), (1,)), ((), ())), preferred_element_type=F32
            )
            scores = scores + bias_ref[...]
            top = jnp.max(scores, axis=1, keepdims=True)
            if not first:
                before = carry[0][head][:, :1]
                top = jnp.maximum(top, before)
            weights = jnp.exp2((scores - top) * factor)
            total = jnp.sum(weights, axis=1, keepdims=True)
            mixed = jnp.dot(weights.astype(BF), value, preferred_element_type=F32)
            if not first:
                keep = jnp.exp2((before - top) * factor)
                total = total + carry[1][head][:, :1] * keep
                mixed = mixed + carry[2][head] * keep
            if last:
                outs[0][:, head * width : (head + 1) * width] = (mixed / total).astype(BF)
            else:
                outs[0][head] = jnp.broadcast_to(top, (tokens, width))
                outs[1][head] = jnp.broadcast_to(total, (tokens, width))
                outs[2][head] = mixed


def attend(carry, last, head_groups, q, kv, place, low, high):
    heads, tokens, width = q.shape
    count = kv.shape[0] * tokens
    first = carry is None
    part = jax.ShapeDtypeStruct((heads, tokens, width), F32)
    whole = jax.ShapeDtypeStruct((tokens, heads * width), BF)
    return pl.pallas_call(
        lambda *refs: attend_kernel(first, last, head_groups, *refs),
        out_shape=whole if last else [part, part, part],
        scratch_shapes=[pltpu.VMEM((tokens, count), F32)],
        compiler_params=pltpu.CompilerParams(vmem_limit_bytes=14 * 1024 * 1024 + 5 * tokens * count * 4),
        cost_estimate=CHEAP,
    )(q, kv, place, low, high, *(() if first else carry))


def call(kernel, out_shape, *operands, head=None):
    size = sum(x.size * x.dtype.itemsize for x in jax.tree.leaves((operands, out_shape)))
    vmem = pl.BlockSpec(memory_space=pltpu.VMEM)
    in_specs = [vmem] * len(operands)
    if head is not None:
        in_specs = [pl.BlockSpec(memory_space=pltpu.SMEM)] + in_specs
        operands = (head.reshape(1), *operands)
    return pl.pallas_call(
        kernel,
        out_shape=out_shape,
        in_specs=in_specs,
        out_specs=jax.tree.map(lambda _: vmem, out_shape),
        compiler_params=pltpu.CompilerParams(vmem_limit_bytes=size + 6 * 1024 * 1024),
        cost_estimate=CHEAP,
    )(*operands)


def contract(rows, weight, flipped):
    dims = (((1,), (1 if flipped else 0,)), ((), ()))
    return lax.dot_general(rows, weight, dims, preferred_element_type=F32)


def flat(ref, expert):
    blocks, rows, width = ref.shape[1:]
    return ref[expert].reshape(blocks * rows, width)


def features_of(half, refs):
    count = refs[0].shape[1 if len(refs) == 2 else 2] // 2
    return pl.ds(pl.multiple_of(half * count, count), count)


def to_hidden(rows, refs, e, half):
    spot = features_of(half, refs)
    if len(refs) == 2:
        made = [contract(rows, ref[e, spot, :], False) for ref in refs]
        return jnp.concatenate(made, axis=1)
    return contract(rows, refs[0][e, :, spot], True)


def from_hidden(rows, refs, e, half):
    spot = features_of(half, refs)
    if len(refs) == 2:
        width = refs[0].shape[2]
        made = [
            contract(rows[:, n * width : (n + 1) * width], refs[n][e, spot, :], True)
            for n in range(2)
        ]
        return made[0] + made[1]
    return contract(rows, refs[0][e, :, spot], False)


def hidden_width(weights):
    return weights[0].shape[2] * 2 if len(weights) == 2 else weights[0].shape[1]


def dispatch(matrix, level):
    count, side, rows, _ = matrix.shape
    width = level[0].shape[1]

    def kernel(matrix_ref, *refs):
        for a in range(side):
            rows_in = refs[a][...]
            for e in range(count):
                refs[-1][e, a] = contract(matrix_ref[e, a], rows_in, False).astype(BF)

    shape = jax.ShapeDtypeStruct((count, side, rows, width), BF)
    return call(kernel, shape, matrix, *level)


def project(heads, weight):
    rows, width = heads.shape[0], weight.shape[1]

    def kernel(heads_ref, weight_ref, out_ref, send_ref):
        step = 512
        for at in range(0, width, step):
            made = contract(heads_ref[...], weight_ref[:, at : at + step], False)
            out_ref[:, at : at + step] = made
            send_ref[:, at : at + step] = made.astype(BF)

    shapes = [jax.ShapeDtypeStruct((rows, width), kind) for kind in (F32, BF)]
    return call(kernel, shapes, heads, weight)


def normalize(head, inputs, other_inputs, made, arrived, gain):
    rows, width = inputs.shape

    def kernel(head_ref, in_ref, other_ref, made_ref, arrived_ref, gain_ref, *outs):
        def stream_of(ref, half):
            lanes = pl.ds(pl.multiple_of(half * width, width), width)
            added = made_ref[:, lanes] + arrived_ref[:, lanes].astype(F32)
            return (ref[...].astype(F32) + added).astype(BF)

        stream = stream_of(in_ref, head_ref[0])
        wide = stream.astype(F32)
        other = stream_of(other_ref, 1 - head_ref[0]).astype(F32)
        squares = jnp.sum(wide * wide + other * other, axis=1, keepdims=True)
        inverse = lax.rsqrt(squares / D + 1e-06)
        outs[0][...] = (wide * inverse * gain_ref[...].astype(F32)).astype(BF)
        outs[1][...] = stream
        outs[2][...] = inverse

    shapes = [
        jax.ShapeDtypeStruct((rows, width), BF),
        jax.ShapeDtypeStruct((rows, width), BF),
        jax.ShapeDtypeStruct((rows, 1), F32),
    ]
    return call(kernel, shapes, inputs, other_inputs, made, arrived, gain, head=head)


def half_hidden(head, own, other, weights):
    count, side, rows, _ = own.shape
    width = hidden_width(weights)

    def kernel(head_ref, own_ref, other_ref, *refs):
        refs, outs = refs[:-2], refs[-2:]
        for e in range(count):
            mine = to_hidden(flat(own_ref, e), refs, e, head_ref[0])
            outs[0][e] = mine.reshape(side, rows, width)
            theirs = to_hidden(flat(other_ref, e), refs, e, 1 - head_ref[0])
            outs[1][e] = theirs.reshape(side, rows, width)

    shape = jax.ShapeDtypeStruct((count, side, rows, width), F32)
    return call(kernel, [shape, shape], own, other, *weights, head=head)


def sum_hidden(half, own_refs, other_refs, refs, out_ref, e, start):
    side, rows = out_ref.shape[1], out_ref.shape[3]
    for b in range(side):
        if start is not None and b == 0:
            out_ref[e, 0] = start[0][e]
        else:
            made = to_hidden(flat(own_refs[b], e), refs, e, half)
            out_ref[e, b] = made.reshape(side, rows, made.shape[1])
    for a in range(side):
        if start is not None and a == 0:
            made = flat(start[1], e)
        else:
            made = to_hidden(flat(other_refs[a], e), refs, e, 1 - half)
        for b in range(side):
            out_ref[e, b, a] += made[b * rows : (b + 1) * rows]


def whole_hidden(head, own, other, weights):
    side = len(own)
    count, _, rows, _ = own[0].shape

    def kernel(head_ref, *refs):
        own_refs, other_refs = refs[:side], refs[side : 2 * side]
        for e in range(count):
            sum_hidden(
                head_ref[0], own_refs, other_refs, refs[2 * side : -1], refs[-1], e, None
            )

    shape = jax.ShapeDtypeStruct((count, side, side, rows, hidden_width(weights)), F32)
    return call(kernel, shape, *own, *other, *weights, head=head)


def column(ref, e, a):
    side, rows, width = ref.shape[2:]
    return ref[e, a].reshape(side * rows, width)


def send_column(head_ref, rows_ref, refs, outs, k):
    for e in range(rows_ref.shape[0]):
        made = from_hidden(column(rows_ref, e, k), refs, e, 1 - head_ref[0])
        outs[k][e] = made.astype(BF).reshape(outs[k].shape[1:])


def forward(head, own, other, start, weights, down):
    side = len(own) + 1
    count, _, rows, features = own[0].shape
    width = hidden_width(weights)
    half = width // 2

    def kernel(head_ref, *refs):
        refs = list(refs)
        own_refs = [None] + [refs.pop(0) for _ in range(side - 1)]
        other_refs = [None] + [refs.pop(0) for _ in range(side - 1)]
        begin = [refs.pop(0), refs.pop(0)]
        weight_refs = [refs.pop(0), refs.pop(0)]
        down_ref, hidden_ref, units_ref = refs[:3]
        for e in range(count):
            sum_hidden(head_ref[0], own_refs, other_refs, weight_refs, hidden_ref, e, begin)
            for a in range(side):
                for b in range(side):
                    gate = hidden_ref[e, b, a, :, :half]
                    upper = hidden_ref[e, b, a, :, half:]
                    silu = gate / (1.0 + jnp.exp(-gate))
                    units_ref[e, a, b] = (silu * upper).astype(BF)
        for k in range(side - 1, -1, -1):
            send_column(head_ref, units_ref, [down_ref], refs[3:], k)

    shapes = [
        jax.ShapeDtypeStruct((count, side, side, rows, width), F32),
        jax.ShapeDtypeStruct((count, side, side, rows, half), BF),
    ] + [jax.ShapeDtypeStruct((count, side, rows, features), BF)] * side
    made = call(kernel, shapes, *own, *other, *start, *weights, down, head=head)
    return made[0], made[1], made[2:]


def backward(head, hidden, units_grad, weights):
    count, side, _, rows, width = hidden.shape
    half = width // 2
    features = weights[0].shape[1] // 2

    def kernel(head_ref, hidden_ref, grad_ref, gate_ref, up_ref, both_ref, *outs):
        for e in range(count):
            for a in range(side):
                for b in range(side):
                    gate = hidden_ref[e, b, a, :, :half]
                    upper = hidden_ref[e, b, a, :, half:]
                    grad = grad_ref[e, b, a]
                    sigmoid = 1.0 / (1.0 + jnp.exp(-gate))
                    slope = sigmoid * (1.0 + gate * (1.0 - sigmoid))
                    both_ref[e, a, b, :, :half] = (grad * upper * slope).astype(BF)
                    both_ref[e, a, b, :, half:] = (grad * (gate * sigmoid)).astype(BF)
        for k in range(side - 1, -1, -1):
            send_column(head_ref, both_ref, [gate_ref, up_ref], outs, k)

    shapes = [jax.ShapeDtypeStruct((count, side, side, rows, width), BF)] + [
        jax.ShapeDtypeStruct((count, side, rows, features), BF)
    ] * side
    made = call(kernel, shapes, hidden, units_grad, *weights, head=head)
    return made[0], made[1:]


def finish(head, rows, weights, arrived, k):
    count, side = rows.shape[:2]

    def kernel(head_ref, rows_ref, *refs):
        for e in range(count):
            mine = jnp.concatenate([rows_ref[e, a, k] for a in range(side)], axis=0)
            made = from_hidden(mine, refs[:-2], e, head_ref[0]) + flat(refs[-2], e).astype(F32)
            refs[-1][e] = made.astype(BF).reshape(refs[-1].shape[1:])

    shape = jax.ShapeDtypeStruct(arrived.shape, BF)
    return call(kernel, shape, rows, *weights, arrived, head=head)


def weight_grad(head, units, own, other):
    side = len(own)
    count, _, _, rows, width = units.shape
    features = own[0].shape[3]

    def kernel(head_ref, units_ref, *refs):
        own_refs, other_refs, out_ref = refs[:side], refs[side : 2 * side], refs[-1]
        dims = (((0,), (0,)), ((), ()))
        spot = pl.multiple_of(head_ref[0] * features, features)
        away = pl.multiple_of((1 - head_ref[0]) * features, features)
        for e in range(count):
            by_own = [units_ref[e, a, b] for b in range(side) for a in range(side)]
            by_other = [units_ref[e, a, b] for a in range(side) for b in range(side)]
            for order, refs_of, lane in ((by_own, own_refs, spot), (by_other, other_refs, away)):
                left = jnp.concatenate(order, axis=0)
                right = jnp.concatenate([flat(ref, e) for ref in refs_of], axis=0)
                made = lax.dot_general(left, right, dims, preferred_element_type=F32)
                out_ref[e, :, pl.ds(lane, features)] = made.astype(BF)

    shape = jax.ShapeDtypeStruct((count, width, 2 * features), BF)
    return call(kernel, shape, units, *own, *other, head=head)


def local(
    inputs,
    queries,
    keys,
    values,
    lengths,
    out_weight,
    norm_gain,
    expert_ids,
    gate_codes,
    gate_weight,
    up_weight,
    down_weight,
    cotangent,
):
    devices = lax.axis_size("ctx")
    position = lax.axis_index("ctx")
    head = lax.axis_index("head")
    deep, side = grid_of(devices)
    plane = side * side

    def swap(rows):
        return swap_cores(rows, devices)

    def z_masks(k):
        return (k * plane, k * plane)

    def a_masks(k):
        return (k, k * side)

    def b_masks(k):
        return (k * side, k)

    def along(array, masks_of, count):
        return [array] + [exchange(array, devices, masks_of(k)) for k in range(1, count)]

    local_tokens, local_heads, head_width = queries.shape
    kv_heads = keys.shape[1]
    head_groups = local_heads // kv_heads
    half_width = inputs.shape[1]
    capacity = max(2, 5 * TOK_DEV * TOP // (4 * EXP_DEV * devices))
    tokens = deep * local_tokens
    block_rows = -(-deep * capacity // 16) * 16

    joint = (gate_weight, up_weight)

    packed = jnp.concatenate(
        [
            keys.transpose(1, 0, 2).reshape(kv_heads * local_tokens, head_width),
            values.transpose(1, 0, 2).reshape(kv_heads * local_tokens, head_width),
            expert_ids.T.astype(BF),
            gate_codes.T.astype(BF),
        ],
        axis=0,
    )
    pack_z = jnp.stack(along(packed, z_masks, deep))
    pack_a = jnp.stack(along(pack_z, a_masks, side))
    pack_b = along(pack_a, b_masks, side)
    chunks = devices

    order = jnp.arange(chunks, dtype=jnp.int32)
    z_part, a_part, b_part = order % deep, order // deep % side, order // (deep * side)
    shift = jnp.where(head == 0, a_part + b_part * side, a_part * side + b_part)
    sources = position ^ (z_part * plane + shift)

    def places_of(owner):
        within = jnp.arange(local_tokens, dtype=jnp.int32)
        half = local_tokens // 2
        owner = owner[..., None]
        return jnp.where(
            within < half, owner * half + within, (2 * devices - 1 - owner) * half + within - half
        )

    docs_in = lengths.shape[0]
    upto = jnp.arange(docs_in)[:, None] <= jnp.arange(docs_in)[None, :]
    ends = jnp.sum(jnp.where(upto, lengths[:, None], 0), axis=0)
    high = places_of(position[None])[0][:, None]
    low = jnp.max(jnp.where(high >= ends[None, :], ends[None, :], 0), axis=1, keepdims=True)
    key_places = places_of(sources).reshape(side, 1, side * deep * local_tokens)
    grouped = queries.transpose(1, 0, 2)
    carry = None
    for k in range(side):
        part = pack_b[k].reshape(side * deep, *packed.shape)
        carry = attend(carry, k == side - 1, head_groups, grouped, part, key_places[k], low, high)
    heads = carry

    upstream = cotangent.astype(F32)
    cot_z = along(after(cotangent, pack_z), z_masks, deep)
    cot_z = jnp.stack(after(tuple(cot_z), heads)).reshape(tokens, half_width)
    heads = after(heads, cot_z)
    cot_a = along(cot_z, a_masks, side)

    made, made_bf = project(heads, out_weight)
    arrived = swap(made_bf)
    normed, stream, inverse = normalize(
        head, inputs, swap(inputs), made, arrived, norm_gain.reshape(1, half_width)
    )
    wide = stream.astype(F32)
    gain = norm_gain.astype(F32)

    near = pack_a[..., -2 * TOP :, :].astype(jnp.int32)
    near_ids, near_codes = near[..., :TOP, :], near[..., TOP:, :].astype(F32)
    near_total = jnp.sum(near_codes, axis=-2)
    owners = position ^ (jnp.arange(side, dtype=jnp.int32) * jnp.where(head == 0, side, 1))
    experts = owners[:, None] * EXP_DEV + jnp.arange(EXP_DEV, dtype=jnp.int32)
    hit = near_ids == experts[:, :, None, None, None, None]
    share = jnp.sum(jnp.where(hit, near_codes, 0.0), axis=-2) / near_total
    member = jnp.any(hit, axis=-2)
    before = jnp.arange(local_tokens)[:, None] < jnp.arange(local_tokens)[None, :]
    rank = jnp.einsum(
        "keazt,tu->keazu", member.astype(BF), before.astype(BF), preferred_element_type=F32
    ).astype(jnp.int32)
    slot = jnp.arange(deep, dtype=jnp.int32)[:, None] * capacity + rank
    slot = jnp.where(member, slot, -1)
    slot = slot.reshape(side, EXP_DEV, side, tokens)
    share = share.reshape(side, EXP_DEV, side, tokens)
    hot = slot[..., None, :] == jnp.arange(block_rows, dtype=jnp.int32)[:, None]
    hot_share = jnp.where(hot, share[..., None, :], 0.0).astype(BF)
    hot = hot.astype(BF)

    def to_b(rows):
        return [None] + [exchange(rows[k], devices, b_masks(k)) for k in range(1, side)]

    def return_rows(total, matrix, arrived):
        got = [total[0]] + list(arrived)

        def dense(a):
            out = 0.0
            for k in range(side):
                out = out + jnp.einsum(
                    "eru,erd->ud", matrix[k, :, a], got[k][:, a], preferred_element_type=F32
                )
            return out

        arrived = [exchange(dense(k).astype(BF), devices, a_masks(k)) for k in range(1, side)]
        near_sum = dense(0)
        for rows in arrived:
            near_sum = near_sum + rows.astype(F32)
        near_sum = near_sum.reshape(deep, local_tokens, half_width)
        across = [
            exchange(near_sum[k].astype(BF), devices, z_masks(k)) for k in range(1, deep)
        ]
        return arrived, near_sum, across

    def last_sum(near_sum, across):
        result = near_sum[0]
        for rows in across:
            result = result + rows.astype(F32)
        return result

    norm_z = along(normed, z_masks, deep)
    cot_a = list(after(tuple(cot_a), normed))
    cot_out = [dispatch(hot_share[k], cot_a) for k in range(side)]
    cot_b = to_b(cot_out)
    norm_z = jnp.stack(after(tuple(norm_z), *cot_out)).reshape(tokens, half_width)
    norm_a = along(norm_z, a_masks, side)
    incoming = [cot_out[0]] + cot_b[1:]
    incoming_other = [swap(rows) for rows in incoming]
    norm_out = [None] + [dispatch(hot[k], norm_a) for k in range(1, side)]
    norm_b = to_b(norm_out)
    norm_out[0] = dispatch(after(hot[0], norm_out[1:]), norm_a)
    start = half_hidden(head, norm_out[0], swap(norm_out[0]), joint)
    units_grad = whole_hidden(head, incoming, incoming_other, (down_weight,))
    own_rows = list(after(tuple(norm_b[1:]), units_grad, *start))
    other_rows = [swap(rows) for rows in own_rows]
    hidden, units, theirs = forward(head, own_rows, other_rows, start, joint, down_weight)

    total = [None] * side
    for k in range(side - 1, -1, -1):
        total[k] = finish(head, units, (down_weight,), swap(theirs[k]), k)
    sent = to_b(total)[1:]
    both, theirs = backward(head, after(hidden, *total), units_grad, joint)
    back_total = [None] * side
    for k in range(side - 1, -1, -1):
        back_total[k] = finish(head, both, joint, swap(theirs[k]), k)
    sent = after(tuple(sent), *back_total)
    arrived, near_sum, across = return_rows(total, hot_share, sent)
    mixture = last_sum(near_sum, across)
    output = (wide + mixture).astype(BF)
    back_total = list(after(tuple(back_total), *arrived))
    back_sent = to_b(back_total)[1:]
    back_sent = list(after(tuple(back_sent), output))
    _, back_sum, back_across = return_rows(back_total, hot, back_sent)
    down_grad = weight_grad(head, after(units, back_sum), incoming, incoming_other)
    scaled = last_sum(back_sum, after(tuple(back_across), down_grad)) * gain
    inner = lax.psum(jnp.sum(scaled * wide, axis=1), "head")[:, None]
    input_grad = (upstream + inverse * scaled - wide * inverse**3 * inner / D).astype(BF)
    norm_term = (inverse**2 * inner / D**0.5)[:, 0]
    return (output, input_grad, down_grad, norm_term)


def solution(mesh):
    in_specs = (
        P("ctx", "head"),
        P("ctx", "head", None),
        P("ctx", "head", None),
        P("ctx", "head", None),
        P(),
        P("head", None),
        P("head"),
        P("ctx", None),
        P("ctx", None),
        P("ctx", None, "head"),
        P("ctx", None, "head"),
        P("ctx", "head", None),
        P("ctx", "head"),
    )
    out_specs = (P("ctx", "head"), P("ctx", "head"), P("ctx", "head", None), P("ctx"))
    return jax.shard_map(local, mesh=mesh, in_specs=in_specs, out_specs=out_specs, check_vma=False)
```

```python
import jax
import jax.numpy as jnp
from jax import lax
from jax.experimental import pallas as pl
from jax.experimental.pallas import tpu as pltpu
from jax.sharding import PartitionSpec as P

D = 2048
TOP = 8
EXP_DEV = 2
TOK_DEV = 128
BF = jnp.bfloat16
F32 = jnp.float32
AXES = ("ctx", "head")
CHEAP = pl.CostEstimate(flops=1, bytes_accessed=1, transcendentals=0)


def grid_of(devices):
    side = 2 if devices < 64 else 4
    return devices // (side * side), side


def exchange(array, devices, masks):
    pairs = [
        (c * 2 + h, (c ^ masks[h]) * 2 + h) for c in range(devices) for h in range(2)
    ]
    return lax.ppermute(array, AXES, pairs)


def swap_cores(array, devices):
    pairs = [(c * 2 + h, c * 2 + 1 - h) for c in range(devices) for h in range(2)]
    return lax.ppermute(array, AXES, pairs)


LOG2E = 1.4426950408889634


def after(value, *others):
    return lax.optimization_barrier((value, others))[0]


def attend_heads(head_groups, q_ref, kv_ref, place_ref, low_ref, high_ref, bias_ref, made_ref):
    heads, tokens, width = q_ref.shape
    chunks = kv_ref.shape[0]
    count = chunks * tokens
    kv_heads = heads // head_groups
    place = place_ref[...]
    seen = (place >= low_ref[...]) & (place <= high_ref[...])
    bias_ref[...] = jnp.where(seen, 0.0, -1e30)
    factor = width ** (-0.5) * LOG2E
    for kv in range(kv_heads):
        key = kv_ref[:, kv * tokens : (kv + 1) * tokens, :].reshape(count, width)
        start = (kv_heads + kv) * tokens
        value = kv_ref[:, start : start + tokens, :].reshape(count, width)
        for group in range(head_groups):
            head = kv * head_groups + group
            scores = lax.dot_general(
                q_ref[head], key, (((1,), (1,)), ((), ())), preferred_element_type=F32
            )
            scores = scores + bias_ref[...]
            top = jnp.max(scores, axis=1, keepdims=True)
            weights = jnp.exp2((scores - top) * factor)
            total = jnp.sum(weights, axis=1, keepdims=True)
            mixed = jnp.dot(weights.astype(BF), value, preferred_element_type=F32)
            made_ref[head, :, :width] = jnp.broadcast_to(top, (tokens, width))
            made_ref[head, :, width : 2 * width] = jnp.broadcast_to(total, (tokens, width))
            made_ref[head, :, 2 * width :] = mixed


def merge_heads(first_ref, second_ref, head, width):
    factor = width ** (-0.5) * LOG2E
    parts = []
    for ref in (first_ref, second_ref):
        parts.append([ref[head, :, n * width : (n + 1) * width] for n in range(3)])
    top = jnp.maximum(parts[0][0], parts[1][0])
    keep = [jnp.exp2((part[0] - top) * factor) for part in parts]
    total = parts[0][1] * keep[0] + parts[1][1] * keep[1]
    mixed = parts[0][2] * keep[0] + parts[1][2] * keep[1]
    return top, total, mixed


def attend(carry, head_groups, q, kv, place, low, high):
    heads, tokens, width = q.shape
    count = kv.shape[0] * tokens
    wide = 3 * width
    first = carry is None

    def kernel(*refs):
        out_ref, bias_ref, made_ref, held_ref, sems, held_sem = refs[-6:]
        if not first:
            held_copy = pltpu.make_async_copy(refs[5], held_ref, held_sem)
            held_copy.start()
        attend_heads(head_groups, *refs[:5], bias_ref, made_ref)
        if not first:
            held_copy.wait()
            for head in range(heads):
                merged = merge_heads(held_ref, made_ref, head, width)
                for n in range(3):
                    made_ref[head, :, n * width : (n + 1) * width] = merged[n]
        copy = pltpu.make_async_copy(made_ref, out_ref, sems)
        copy.start()
        copy.wait()

    vmem, far = pl.BlockSpec(memory_space=pltpu.VMEM), pl.BlockSpec(memory_space=pltpu.HBM)
    carry_shape = (heads, tokens, wide)
    return pl.pallas_call(
        kernel,
        out_shape=jax.ShapeDtypeStruct(carry_shape, F32),
        in_specs=[vmem] * 5 + ([] if first else [far]),
        out_specs=far,
        scratch_shapes=[
            pltpu.VMEM((tokens, count), F32),
            pltpu.VMEM(carry_shape, F32),
            pltpu.VMEM((8, 128) if first else carry_shape, F32),
            pltpu.SemaphoreType.DMA,
            pltpu.SemaphoreType.DMA,
        ],
        compiler_params=pltpu.CompilerParams(vmem_limit_bytes=(18 << 20) + 5 * tokens * count * 4),
        cost_estimate=CHEAP,
    )(q, kv, place, low, high, *(() if first else (carry,)))


def attend_and_project(carry, head_groups, q, kv, place, low, high, weight):
    heads, tokens, width = q.shape
    count = kv.shape[0] * tokens
    features = weight.shape[1]
    pieces = 4
    rows = weight.shape[0] // pieces

    def kernel(*refs):
        carry_ref, weight_ref, out_ref, send_ref = refs[5:9]
        bias_ref, held, made_ref, weight_held, heads_ref, held_sem, weight_sems = refs[9:]
        held_copy = pltpu.make_async_copy(carry_ref, held, held_sem)
        held_copy.start()
        copies = []
        for n in range(pieces):
            at = pl.ds(n * rows, rows)
            copies.append(
                pltpu.make_async_copy(weight_ref.at[at], weight_held.at[at], weight_sems.at[n])
            )
            copies[n].start()
        attend_heads(head_groups, *refs[:5], bias_ref, made_ref)
        held_copy.wait()
        for head in range(heads):
            _, total, mixed = merge_heads(held, made_ref, head, width)
            heads_ref[:, head * width : (head + 1) * width] = (mixed / total).astype(BF)
        for copy in copies:
            copy.wait()
        step = 512
        for at in range(0, features, step):
            made = contract(heads_ref[...], weight_held[:, at : at + step], False)
            out_ref[:, at : at + step] = made
            send_ref[:, at : at + step] = made.astype(BF)

    vmem, far = pl.BlockSpec(memory_space=pltpu.VMEM), pl.BlockSpec(memory_space=pltpu.HBM)
    return pl.pallas_call(
        kernel,
        out_shape=[jax.ShapeDtypeStruct((tokens, features), kind) for kind in (F32, BF)],
        in_specs=[vmem] * 5 + [far] * 2,
        out_specs=[vmem, vmem],
        scratch_shapes=[
            pltpu.VMEM((tokens, count), F32),
            pltpu.VMEM(carry.shape, F32),
            pltpu.VMEM(carry.shape, F32),
            pltpu.VMEM(weight.shape, BF),
            pltpu.VMEM((tokens, heads * width), BF),
            pltpu.SemaphoreType.DMA,
            pltpu.SemaphoreType.DMA((pieces,)),
        ],
        compiler_params=pltpu.CompilerParams(vmem_limit_bytes=58 << 20),
        cost_estimate=CHEAP,
    )(q, kv, place, low, high, carry, weight)


def call(kernel, out_shape, *operands, head=None):
    size = sum(x.size * x.dtype.itemsize for x in jax.tree.leaves((operands, out_shape)))
    vmem = pl.BlockSpec(memory_space=pltpu.VMEM)
    in_specs = [vmem] * len(operands)
    if head is not None:
        in_specs = [pl.BlockSpec(memory_space=pltpu.SMEM)] + in_specs
        operands = (head.reshape(1), *operands)
    return pl.pallas_call(
        kernel,
        out_shape=out_shape,
        in_specs=in_specs,
        out_specs=jax.tree.map(lambda _: vmem, out_shape),
        compiler_params=pltpu.CompilerParams(vmem_limit_bytes=size + 6 * 1024 * 1024),
        cost_estimate=CHEAP,
    )(*operands)


def contract(rows, weight, flipped):
    dims = (((1,), (1 if flipped else 0,)), ((), ()))
    return lax.dot_general(rows, weight, dims, preferred_element_type=F32)


def flat(ref, expert):
    blocks, rows, width = ref.shape[1:]
    return ref[expert].reshape(blocks * rows, width)


def features_of(half, refs):
    count = refs[0].shape[1 if len(refs) == 2 else 2] // 2
    return pl.ds(pl.multiple_of(half * count, count), count)


def to_hidden(rows, refs, e, half):
    spot = features_of(half, refs)
    if len(refs) == 2:
        made = [contract(rows, ref[e, spot, :], False) for ref in refs]
        return jnp.concatenate(made, axis=1)
    return contract(rows, refs[0][e, :, spot], True)


def from_hidden(rows, refs, e, half):
    spot = features_of(half, refs)
    if len(refs) == 2:
        width = refs[0].shape[2]
        made = [
            contract(rows[:, n * width : (n + 1) * width], refs[n][e, spot, :], True)
            for n in range(2)
        ]
        return made[0] + made[1]
    return contract(rows, refs[0][e, :, spot], False)


def hidden_width(weights):
    return weights[0].shape[2] * 2 if len(weights) == 2 else weights[0].shape[1]


def dispatch(matrix, level):
    count, side, rows, _ = matrix.shape
    width = level[0].shape[1]

    def kernel(matrix_ref, *refs):
        for a in range(side):
            rows_in = refs[a][...]
            for e in range(count):
                refs[-1][e, a] = contract(matrix_ref[e, a], rows_in, False).astype(BF)

    shape = jax.ShapeDtypeStruct((count, side, rows, width), BF)
    return call(kernel, shape, matrix, *level)


def normalize(head, inputs, other_inputs, made, arrived, gain):
    rows, width = inputs.shape

    def kernel(head_ref, in_ref, other_ref, made_ref, arrived_ref, gain_ref, *outs):
        def stream_of(ref, half):
            lanes = pl.ds(pl.multiple_of(half * width, width), width)
            added = made_ref[:, lanes] + arrived_ref[:, lanes].astype(F32)
            return (ref[...].astype(F32) + added).astype(BF)

        stream = stream_of(in_ref, head_ref[0])
        wide = stream.astype(F32)
        other = stream_of(other_ref, 1 - head_ref[0]).astype(F32)
        squares = jnp.sum(wide * wide + other * other, axis=1, keepdims=True)
        inverse = lax.rsqrt(squares / D + 1e-06)
        outs[0][...] = (wide * inverse * gain_ref[...].astype(F32)).astype(BF)
        outs[1][...] = stream
        outs[2][...] = inverse

    shapes = [
        jax.ShapeDtypeStruct((rows, width), BF),
        jax.ShapeDtypeStruct((rows, width), BF),
        jax.ShapeDtypeStruct((rows, 1), F32),
    ]
    return call(kernel, shapes, inputs, other_inputs, made, arrived, gain, head=head)


def half_hidden(head, own, other, weights):
    count, side, rows, _ = own.shape
    width = hidden_width(weights)

    def kernel(head_ref, own_ref, *refs):
        other_refs, refs, outs = refs[:count], refs[count:-2], refs[-2:]
        for e in range(count):
            mine = to_hidden(flat(own_ref, e), refs, e, head_ref[0])
            outs[0][e] = mine.reshape(side, rows, width)
            theirs = to_hidden(flat(other_refs[e], 0), refs, e, 1 - head_ref[0])
            outs[1][e] = theirs.reshape(side, rows, width)

    shape = jax.ShapeDtypeStruct((count, side, rows, width), F32)
    return call(kernel, [shape, shape], own, *other, *weights, head=head)


def sum_hidden(half, own_refs, other_refs, refs, out_ref, e, start):
    side, rows = out_ref.shape[1], out_ref.shape[3]
    for b in range(side):
        if start is not None and b == 0:
            out_ref[e, 0] = start[0][e]
        else:
            made = to_hidden(flat(own_refs[b], e), refs, e, half)
            out_ref[e, b] = made.reshape(side, rows, made.shape[1])
    for a in range(side):
        if start is not None and a == 0:
            made = flat(start[1], e)
        else:
            made = to_hidden(flat(other_refs[a], e), refs, e, 1 - half)
        for b in range(side):
            out_ref[e, b, a] += made[b * rows : (b + 1) * rows]


def whole_hidden(head, own, other, weights):
    side = len(own)
    count, _, rows, _ = own[0].shape

    def kernel(head_ref, *refs):
        own_refs, other_refs = refs[:side], refs[side : 2 * side]
        for e in range(count):
            sum_hidden(
                head_ref[0], own_refs, other_refs, refs[2 * side : -1], refs[-1], e, None
            )

    shape = jax.ShapeDtypeStruct((count, side, side, rows, hidden_width(weights)), F32)
    return call(kernel, shape, *own, *other, *weights, head=head)


def column(ref, e, a):
    side, rows, width = ref.shape[2:]
    return ref[e, a].reshape(side * rows, width)


def send_column(head_ref, rows_ref, refs, outs, k):
    for e in range(rows_ref.shape[0]):
        made = from_hidden(column(rows_ref, e, k), refs, e, 1 - head_ref[0])
        outs[k][e] = made.astype(BF).reshape(outs[k].shape[1:])


def forward(head, own, other, start, weights, down):
    side = len(own) + 1
    count, _, rows, features = own[0].shape
    width = hidden_width(weights)
    half = width // 2

    def kernel(head_ref, *refs):
        refs = list(refs)
        own_refs = [None] + [refs.pop(0) for _ in range(side - 1)]
        other_refs = [None] + [refs.pop(0) for _ in range(side - 1)]
        begin = [refs.pop(0), refs.pop(0)]
        weight_refs = [refs.pop(0), refs.pop(0)]
        down_ref, hidden_ref, units_ref = refs[:3]
        for e in range(count):
            sum_hidden(head_ref[0], own_refs, other_refs, weight_refs, hidden_ref, e, begin)
            for a in range(side):
                for b in range(side):
                    gate = hidden_ref[e, b, a, :, :half]
                    upper = hidden_ref[e, b, a, :, half:]
                    silu = gate / (1.0 + jnp.exp(-gate))
                    units_ref[e, a, b] = (silu * upper).astype(BF)
        for k in range(side - 1, -1, -1):
            send_column(head_ref, units_ref, [down_ref], refs[3:], k)

    shapes = [
        jax.ShapeDtypeStruct((count, side, side, rows, width), F32),
        jax.ShapeDtypeStruct((count, side, side, rows, half), BF),
    ] + [jax.ShapeDtypeStruct((count, side, rows, features), BF)] * side
    made = call(kernel, shapes, *own, *other, *start, *weights, down, head=head)
    return made[0], made[1], made[2:]


def backward(head, hidden, units_grad, weights):
    count, side, _, rows, width = hidden.shape
    half = width // 2
    features = weights[0].shape[1] // 2

    def kernel(head_ref, hidden_ref, grad_ref, gate_ref, up_ref, both_ref, *outs):
        for e in range(count):
            for a in range(side):
                for b in range(side):
                    gate = hidden_ref[e, b, a, :, :half]
                    upper = hidden_ref[e, b, a, :, half:]
                    grad = grad_ref[e, b, a]
                    sigmoid = 1.0 / (1.0 + jnp.exp(-gate))
                    slope = sigmoid * (1.0 + gate * (1.0 - sigmoid))
                    both_ref[e, a, b, :, :half] = (grad * upper * slope).astype(BF)
                    both_ref[e, a, b, :, half:] = (grad * (gate * sigmoid)).astype(BF)
        for k in range(side - 1, -1, -1):
            send_column(head_ref, both_ref, [gate_ref, up_ref], outs, k)

    shapes = [jax.ShapeDtypeStruct((count, side, side, rows, width), BF)] + [
        jax.ShapeDtypeStruct((count, side, rows, features), BF)
    ] * side
    made = call(kernel, shapes, hidden, units_grad, *weights, head=head)
    return made[0], made[1:]


def finish(head, rows, weights, arrived, k):
    count, side = rows.shape[:2]

    def kernel(head_ref, rows_ref, *refs):
        for e in range(count):
            mine = jnp.concatenate([rows_ref[e, a, k] for a in range(side)], axis=0)
            made = from_hidden(mine, refs[:-2], e, head_ref[0]) + flat(refs[-2], e).astype(F32)
            refs[-1][e] = made.astype(BF).reshape(refs[-1].shape[1:])

    shape = jax.ShapeDtypeStruct(arrived.shape, BF)
    return call(kernel, shape, rows, *weights, arrived, head=head)


def weight_grad(head, units, own, other):
    side = len(own)
    count, _, _, rows, width = units.shape
    features = own[0].shape[3]

    def kernel(head_ref, units_ref, *refs):
        own_refs, other_refs, out_ref = refs[:side], refs[side : 2 * side], refs[-1]
        dims = (((0,), (0,)), ((), ()))
        spot = pl.multiple_of(head_ref[0] * features, features)
        away = pl.multiple_of((1 - head_ref[0]) * features, features)
        for e in range(count):
            by_own = [units_ref[e, a, b] for b in range(side) for a in range(side)]
            by_other = [units_ref[e, a, b] for a in range(side) for b in range(side)]
            for order, refs_of, lane in ((by_own, own_refs, spot), (by_other, other_refs, away)):
                left = jnp.concatenate(order, axis=0)
                right = jnp.concatenate([flat(ref, e) for ref in refs_of], axis=0)
                made = lax.dot_general(left, right, dims, preferred_element_type=F32)
                out_ref[e, :, pl.ds(lane, features)] = made.astype(BF)

    shape = jax.ShapeDtypeStruct((count, width, 2 * features), BF)
    return call(kernel, shape, units, *own, *other, head=head)


def local(
    inputs,
    queries,
    keys,
    values,
    lengths,
    out_weight,
    norm_gain,
    expert_ids,
    gate_codes,
    gate_weight,
    up_weight,
    down_weight,
    cotangent,
):
    devices = lax.axis_size("ctx")
    position = lax.axis_index("ctx")
    head = lax.axis_index("head")
    deep, side = grid_of(devices)
    plane = side * side

    def swap(rows):
        return swap_cores(rows, devices)

    def swap_parts(rows):
        return [swap(rows[e : e + 1]) for e in range(EXP_DEV)]

    def z_masks(k):
        return (k * plane, k * plane)

    def a_masks(k):
        return (k, k * side)

    def b_masks(k):
        return (k * side, k)

    def along(array, masks_of, count):
        return [array] + [exchange(array, devices, masks_of(k)) for k in range(1, count)]

    local_tokens, local_heads, head_width = queries.shape
    kv_heads = keys.shape[1]
    head_groups = local_heads // kv_heads
    half_width = inputs.shape[1]
    capacity = max(2, 5 * TOK_DEV * TOP // (4 * EXP_DEV * devices))
    tokens = deep * local_tokens
    block_rows = -(-deep * capacity // 16) * 16

    joint = (gate_weight, up_weight)

    packed = jnp.concatenate(
        [
            keys.transpose(1, 0, 2).reshape(kv_heads * local_tokens, head_width),
            values.transpose(1, 0, 2).reshape(kv_heads * local_tokens, head_width),
            expert_ids.T.astype(BF),
            gate_codes.T.astype(BF),
        ],
        axis=0,
    )
    pack_z = jnp.stack(along(packed, z_masks, deep))
    pack_a = jnp.stack(along(pack_z, a_masks, side))
    pack_b = along(pack_a, b_masks, side)
    chunks = devices

    order = jnp.arange(chunks, dtype=jnp.int32)
    z_part, a_part, b_part = order % deep, order // deep % side, order // (deep * side)
    shift = jnp.where(head == 0, a_part + b_part * side, a_part * side + b_part)
    sources = position ^ (z_part * plane + shift)

    def places_of(owner):
        within = jnp.arange(local_tokens, dtype=jnp.int32)
        half = local_tokens // 2
        owner = owner[..., None]
        return jnp.where(
            within < half, owner * half + within, (2 * devices - 1 - owner) * half + within - half
        )

    docs_in = lengths.shape[0]
    upto = jnp.arange(docs_in)[:, None] <= jnp.arange(docs_in)[None, :]
    ends = jnp.sum(jnp.where(upto, lengths[:, None], 0), axis=0)
    high = places_of(position[None])[0][:, None]
    low = jnp.max(jnp.where(high >= ends[None, :], ends[None, :], 0), axis=1, keepdims=True)
    key_places = places_of(sources).reshape(side, 1, side * deep * local_tokens)
    grouped = queries.transpose(1, 0, 2)
    carry = None
    for k in range(side - 1):
        part = pack_b[k].reshape(side * deep, *packed.shape)
        carry = attend(carry, head_groups, grouped, part, key_places[k], low, high)
    part = pack_b[-1].reshape(side * deep, *packed.shape)
    made, made_bf = attend_and_project(
        carry, head_groups, grouped, part, key_places[-1], low, high, out_weight
    )

    upstream = cotangent.astype(F32)
    cot_z = along(after(cotangent, pack_z), z_masks, deep)
    cot_z = jnp.stack(after(tuple(cot_z), made_bf)).reshape(tokens, half_width)
    cot_a = along(cot_z, a_masks, side)

    arrived = swap(made_bf)
    normed, stream, inverse = normalize(
        head, inputs, swap(inputs), made, arrived, norm_gain.reshape(1, half_width)
    )
    wide = stream.astype(F32)
    gain = norm_gain.astype(F32)

    near = pack_a[..., -2 * TOP :, :].astype(jnp.int32)
    near_ids, near_codes = near[..., :TOP, :], near[..., TOP:, :].astype(F32)
    near_total = jnp.sum(near_codes, axis=-2)
    owners = position ^ (jnp.arange(side, dtype=jnp.int32) * jnp.where(head == 0, side, 1))
    experts = owners[:, None] * EXP_DEV + jnp.arange(EXP_DEV, dtype=jnp.int32)
    hit = near_ids == experts[:, :, None, None, None, None]
    share = jnp.sum(jnp.where(hit, near_codes, 0.0), axis=-2) / near_total
    member = jnp.any(hit, axis=-2)
    before = jnp.arange(local_tokens)[:, None] < jnp.arange(local_tokens)[None, :]
    rank = jnp.einsum(
        "keazt,tu->keazu", member.astype(BF), before.astype(BF), preferred_element_type=F32
    ).astype(jnp.int32)
    slot = jnp.arange(deep, dtype=jnp.int32)[:, None] * capacity + rank
    slot = jnp.where(member, slot, -1)
    slot = slot.reshape(side, EXP_DEV, side, tokens)
    share = share.reshape(side, EXP_DEV, side, tokens)
    hot = slot[..., None, :] == jnp.arange(block_rows, dtype=jnp.int32)[:, None]
    hot_share = jnp.where(hot, share[..., None, :], 0.0).astype(BF)
    hot = hot.astype(BF)

    def to_b(rows):
        return [None] + [exchange(rows[k], devices, b_masks(k)) for k in range(1, side)]

    def dense(matrix, got, a, lanes):
        out = 0.0
        for k in range(side):
            out = out + jnp.einsum(
                "eru,erd->ud",
                matrix[k, :, a],
                got[k][:, a, :, lanes],
                preferred_element_type=F32,
            )
        return out

    def sum_a(matrix, got, arrived, lanes):
        near_sum = dense(matrix, got, 0, lanes)
        for rows in arrived:
            near_sum = near_sum + rows.astype(F32)
        return near_sum.reshape(deep, local_tokens, near_sum.shape[1])

    def send_a(matrix, got, lanes, waits):
        rows = [dense(matrix, got, k, lanes).astype(BF) for k in range(1, side)]
        rows = after(tuple(rows), waits)
        return [exchange(rows[k - 1], devices, a_masks(k)) for k in range(1, side)]

    def send_z(near_sum):
        return [
            exchange(near_sum[k].astype(BF), devices, z_masks(k)) for k in range(1, deep)
        ]

    def last_sum(near_sum, across):
        result = near_sum[0]
        for rows in across:
            result = result + rows.astype(F32)
        return result

    norm_z = along(normed, z_masks, deep)
    cot_a = list(after(tuple(cot_a), normed))
    cot_out = [dispatch(hot_share[k], cot_a) for k in range(side)]
    cot_b = to_b(cot_out)
    norm_z = jnp.stack(after(tuple(norm_z), *cot_out)).reshape(tokens, half_width)
    norm_a = along(norm_z, a_masks, side)
    incoming = [cot_out[0]] + cot_b[1:]
    incoming_other = [swap(rows) for rows in incoming]
    norm_out = [None] + [dispatch(hot[k], norm_a) for k in range(1, side)]
    norm_b = to_b(norm_out)
    norm_out[0] = dispatch(after(hot[0], norm_out[1:]), norm_a)
    start = half_hidden(head, norm_out[0], swap_parts(norm_out[0]), joint)
    units_grad = whole_hidden(head, incoming, incoming_other, (down_weight,))
    own_rows = list(after(tuple(norm_b[1:]), units_grad, *start))
    other_rows = [swap(rows) for rows in own_rows]
    hidden, units, theirs = forward(head, own_rows, other_rows, start, joint, down_weight)

    total = [None] * side
    for k in range(side - 1, -1, -1):
        total[k] = finish(head, units, (down_weight,), swap(theirs[k]), k)
    sent = to_b(total)[1:]
    both, theirs = backward(head, after(hidden, *total), units_grad, joint)
    back_total = [None] * side
    for k in range(side - 1, -1, -1):
        back_total[k] = finish(head, both, joint, swap(theirs[k]), k)
    sent = after(tuple(sent), both)
    whole = slice(None)
    got = [total[0]] + list(sent)
    arrived = send_a(hot_share, got, whole, ())
    near_sum = sum_a(hot_share, got, arrived, whole)
    across = send_z(near_sum)

    back_total = list(after(tuple(back_total), arrived))
    got = [back_total[0]] + to_b(back_total)[1:]
    quarter = half_width // 2
    lanes = (slice(0, quarter), slice(quarter, half_width))
    arrived = send_a(hot, got, lanes[0], across)
    arrived_next = send_a(hot, got, lanes[1], across)
    back_sum = sum_a(hot, got, arrived, lanes[0])
    back_across = send_z(back_sum)
    back_next = sum_a(hot, got, arrived_next, lanes[1])
    across_next = send_z(back_next)
    output = (wide + last_sum(near_sum, across)).astype(BF)
    down_grad = weight_grad(head, after(units, back_next), incoming, incoming_other)
    scaled = last_sum(back_sum, after(tuple(back_across), back_next))
    scaled_next = last_sum(back_next, after(tuple(across_next), (down_grad, output)))
    scaled = jnp.concatenate([scaled, scaled_next], axis=1) * gain
    inner = jnp.sum(scaled * wide, axis=1, keepdims=True)
    inner = inner + swap(inner)
    input_grad = (upstream + inverse * scaled - wide * inverse**3 * inner / D).astype(BF)
    norm_term = (inverse**2 * inner / D**0.5)[:, 0]
    return (output, input_grad, down_grad, norm_term)


def solution(mesh):
    in_specs = (
        P("ctx", "head"),
        P("ctx", "head", None),
        P("ctx", "head", None),
        P("ctx", "head", None),
        P(),
        P("head", None),
        P("head"),
        P("ctx", None),
        P("ctx", None),
        P("ctx", None, "head"),
        P("ctx", None, "head"),
        P("ctx", "head", None),
        P("ctx", "head"),
    )
    out_specs = (P("ctx", "head"), P("ctx", "head"), P("ctx", "head", None), P("ctx"))
    return jax.shard_map(local, mesh=mesh, in_specs=in_specs, out_specs=out_specs, check_vma=False)
```

```python
import jax
import jax.numpy as jnp
from jax import lax
from jax.experimental import pallas as pl
from jax.experimental.pallas import tpu as pltpu
from jax.sharding import PartitionSpec as P

D = 2048
TOP = 8
EXP_DEV = 2
TOK_DEV = 128
BF = jnp.bfloat16
F32 = jnp.float32
AXES = ("ctx", "head")
CHEAP = pl.CostEstimate(flops=1, bytes_accessed=1, transcendentals=0)


def grid_of(devices):
    side = 2 if devices < 64 else 4
    return devices // (side * side), side


def exchange(array, devices, masks):
    pairs = [
        (c * 2 + h, (c ^ masks[h]) * 2 + h) for c in range(devices) for h in range(2)
    ]
    return lax.ppermute(array, AXES, pairs)


def swap_cores(array, devices):
    pairs = [(c * 2 + h, c * 2 + 1 - h) for c in range(devices) for h in range(2)]
    return lax.ppermute(array, AXES, pairs)


LOG2E = 1.4426950408889634


def after(value, *others):
    return lax.optimization_barrier((value, others))[0]


def attend_heads(head_groups, q_ref, kv_ref, place_ref, low_ref, high_ref, bias_ref, made_ref):
    heads, tokens, width = q_ref.shape
    chunks = kv_ref.shape[0]
    count = chunks * tokens
    kv_heads = heads // head_groups
    place = place_ref[...]
    seen = (place >= low_ref[...]) & (place <= high_ref[...])
    bias_ref[...] = jnp.where(seen, 0.0, -1e30)
    factor = width ** (-0.5) * LOG2E
    for kv in range(kv_heads):
        key = kv_ref[:, kv * tokens : (kv + 1) * tokens, :].reshape(count, width)
        start = (kv_heads + kv) * tokens
        value = kv_ref[:, start : start + tokens, :].reshape(count, width)
        for group in range(head_groups):
            head = kv * head_groups + group
            scores = lax.dot_general(
                q_ref[head], key, (((1,), (1,)), ((), ())), preferred_element_type=F32
            )
            scores = scores + bias_ref[...]
            top = jnp.max(scores, axis=1, keepdims=True)
            weights = jnp.exp2((scores - top) * factor)
            total = jnp.sum(weights, axis=1, keepdims=True)
            mixed = jnp.dot(weights.astype(BF), value, preferred_element_type=F32)
            made_ref[head, :, :width] = jnp.broadcast_to(top, (tokens, width))
            made_ref[head, :, width : 2 * width] = jnp.broadcast_to(total, (tokens, width))
            made_ref[head, :, 2 * width :] = mixed


def merge_heads(first_ref, second_ref, head, width):
    factor = width ** (-0.5) * LOG2E
    parts = []
    for ref in (first_ref, second_ref):
        parts.append([ref[head, :, n * width : (n + 1) * width] for n in range(3)])
    top = jnp.maximum(parts[0][0], parts[1][0])
    keep = [jnp.exp2((part[0] - top) * factor) for part in parts]
    total = parts[0][1] * keep[0] + parts[1][1] * keep[1]
    mixed = parts[0][2] * keep[0] + parts[1][2] * keep[1]
    return top, total, mixed


def attend(carry, head_groups, q, kv, place, low, high):
    heads, tokens, width = q.shape
    count = kv.shape[0] * tokens
    wide = 3 * width
    first = carry is None

    def kernel(*refs):
        out_ref, bias_ref, made_ref, held_ref, sems, held_sem = refs[-6:]
        if not first:
            held_copy = pltpu.make_async_copy(refs[5], held_ref, held_sem)
            held_copy.start()
        attend_heads(head_groups, *refs[:5], bias_ref, made_ref)
        if not first:
            held_copy.wait()
            for head in range(heads):
                merged = merge_heads(held_ref, made_ref, head, width)
                for n in range(3):
                    made_ref[head, :, n * width : (n + 1) * width] = merged[n]
        copy = pltpu.make_async_copy(made_ref, out_ref, sems)
        copy.start()
        copy.wait()

    vmem, far = pl.BlockSpec(memory_space=pltpu.VMEM), pl.BlockSpec(memory_space=pltpu.HBM)
    carry_shape = (heads, tokens, wide)
    return pl.pallas_call(
        kernel,
        out_shape=jax.ShapeDtypeStruct(carry_shape, F32),
        in_specs=[vmem] * 5 + ([] if first else [far]),
        out_specs=far,
        scratch_shapes=[
            pltpu.VMEM((tokens, count), F32),
            pltpu.VMEM(carry_shape, F32),
            pltpu.VMEM((8, 128) if first else carry_shape, F32),
            pltpu.SemaphoreType.DMA,
            pltpu.SemaphoreType.DMA,
        ],
        compiler_params=pltpu.CompilerParams(vmem_limit_bytes=(18 << 20) + 5 * tokens * count * 4),
        cost_estimate=CHEAP,
    )(q, kv, place, low, high, *(() if first else (carry,)))


def attend_and_project(
    half, inputs, other_inputs, carry, head_groups, q, kv, place, low, high, weight
):
    heads, tokens, width = q.shape
    count = kv.shape[0] * tokens
    features = weight.shape[1]
    pieces = 4
    rows = weight.shape[0] // pieces

    def kernel(*refs):
        half_ref, refs = refs[0], refs[1:]
        carry_ref, weight_ref, in_ref, other_ref, out_ref, send_ref = refs[5:11]
        bias_ref, held, made_ref, weight_held, heads_ref, in_held, held_sem, weight_sems, in_sems = (
            refs[11:]
        )
        held_copy = pltpu.make_async_copy(carry_ref, held, held_sem)
        held_copy.start()
        in_copies = [
            pltpu.make_async_copy(ref, in_held.at[n], in_sems.at[n])
            for n, ref in enumerate((in_ref, other_ref))
        ]
        for copy in in_copies:
            copy.start()
        copies = []
        for n in range(pieces):
            at = pl.ds(n * rows, rows)
            copies.append(
                pltpu.make_async_copy(weight_ref.at[at], weight_held.at[at], weight_sems.at[n])
            )
            copies[n].start()
        attend_heads(head_groups, *refs[:5], bias_ref, made_ref)
        held_copy.wait()
        for head in range(heads):
            _, total, mixed = merge_heads(held, made_ref, head, width)
            heads_ref[:, head * width : (head + 1) * width] = (mixed / total).astype(BF)
        for copy in copies:
            copy.wait()
        step = 512
        for at in range(0, features, step):
            made = contract(heads_ref[...], weight_held[:, at : at + step], False)
            out_ref[:, at : at + step] = made
            send_ref[:, at : at + step] = made.astype(BF)
        own = in_ref.shape[1]
        for n, copy in enumerate(in_copies):
            copy.wait()
            side_of = half_ref[0] if n == 0 else 1 - half_ref[0]
            lanes = pl.ds(pl.multiple_of(side_of * own, own), own)
            out_ref[:, lanes] += in_held[n].astype(F32)

    vmem, far = pl.BlockSpec(memory_space=pltpu.VMEM), pl.BlockSpec(memory_space=pltpu.HBM)
    return pl.pallas_call(
        kernel,
        out_shape=[jax.ShapeDtypeStruct((tokens, features), kind) for kind in (F32, BF)],
        in_specs=[pl.BlockSpec(memory_space=pltpu.SMEM)] + [vmem] * 5 + [far] * 4,
        out_specs=[vmem, vmem],
        scratch_shapes=[
            pltpu.VMEM((tokens, count), F32),
            pltpu.VMEM(carry.shape, F32),
            pltpu.VMEM(carry.shape, F32),
            pltpu.VMEM(weight.shape, BF),
            pltpu.VMEM((tokens, heads * width), BF),
            pltpu.VMEM((2, *inputs.shape), BF),
            pltpu.SemaphoreType.DMA,
            pltpu.SemaphoreType.DMA((pieces,)),
            pltpu.SemaphoreType.DMA((2,)),
        ],
        compiler_params=pltpu.CompilerParams(vmem_limit_bytes=58 << 20),
        cost_estimate=CHEAP,
    )(half.reshape(1), q, kv, place, low, high, carry, weight, inputs, other_inputs)


def call(kernel, out_shape, *operands, head=None):
    size = sum(x.size * x.dtype.itemsize for x in jax.tree.leaves((operands, out_shape)))
    vmem = pl.BlockSpec(memory_space=pltpu.VMEM)
    in_specs = [vmem] * len(operands)
    if head is not None:
        in_specs = [pl.BlockSpec(memory_space=pltpu.SMEM)] + in_specs
        operands = (head.reshape(1), *operands)
    return pl.pallas_call(
        kernel,
        out_shape=out_shape,
        in_specs=in_specs,
        out_specs=jax.tree.map(lambda _: vmem, out_shape),
        compiler_params=pltpu.CompilerParams(vmem_limit_bytes=size + 6 * 1024 * 1024),
        cost_estimate=CHEAP,
    )(*operands)


def contract(rows, weight, flipped):
    dims = (((1,), (1 if flipped else 0,)), ((), ()))
    return lax.dot_general(rows, weight, dims, preferred_element_type=F32)


def flat(ref, expert=None):
    blocks, rows, width = ref.shape[-3:]
    return (ref[...] if expert is None else ref[expert]).reshape(blocks * rows, width)


def features_of(half, refs):
    count = refs[0].shape[1 if len(refs) == 2 else 2] // 2
    return pl.ds(pl.multiple_of(half * count, count), count)


def to_hidden(rows, refs, e, half):
    spot = features_of(half, refs)
    if len(refs) == 2:
        made = [contract(rows, ref[e, spot, :], False) for ref in refs]
        return jnp.concatenate(made, axis=1)
    return contract(rows, refs[0][e, :, spot], True)


def from_hidden(rows, refs, e, half):
    spot = features_of(half, refs)
    if len(refs) == 2:
        width = refs[0].shape[2]
        made = [
            contract(rows[:, n * width : (n + 1) * width], refs[n][e, spot, :], True)
            for n in range(2)
        ]
        return made[0] + made[1]
    return contract(rows, refs[0][e, :, spot], False)


def hidden_width(weights):
    return weights[0].shape[2] * 2 if len(weights) == 2 else weights[0].shape[1]


def dispatch(matrix, level, apart):
    count, side, rows, _ = matrix.shape
    width = level[0].shape[1]

    def kernel(matrix_ref, *refs):
        level_refs, outs = refs[:side], refs[side:]
        for e in range(count):
            out_ref = outs[e] if apart else outs[0].at[e]
            for a in range(side):
                out_ref[a] = contract(matrix_ref[e, a], level_refs[a][...], False).astype(BF)

    if apart:
        shapes = [jax.ShapeDtypeStruct((side, rows, width), BF)] * count
    else:
        shapes = [jax.ShapeDtypeStruct((count, side, rows, width), BF)]
    made = call(kernel, shapes, matrix, *level)
    return made if apart else made[0]


def normalize(head, made, arrived, gain):
    rows, width = made.shape[0], gain.shape[1]

    def kernel(head_ref, made_ref, arrived_ref, gain_ref, *outs):
        def stream_of(half):
            lanes = pl.ds(pl.multiple_of(half * width, width), width)
            return (made_ref[:, lanes] + arrived_ref[:, lanes].astype(F32)).astype(BF)

        stream = stream_of(head_ref[0])
        wide = stream.astype(F32)
        other = stream_of(1 - head_ref[0]).astype(F32)
        squares = jnp.sum(wide * wide + other * other, axis=1, keepdims=True)
        inverse = lax.rsqrt(squares / D + 1e-06)
        outs[0][...] = (wide * inverse * gain_ref[...].astype(F32)).astype(BF)
        outs[1][...] = stream
        outs[2][...] = inverse

    shapes = [
        jax.ShapeDtypeStruct((rows, width), BF),
        jax.ShapeDtypeStruct((rows, width), BF),
        jax.ShapeDtypeStruct((rows, 1), F32),
    ]
    return call(kernel, shapes, made, arrived, gain, head=head)


def half_hidden(head, own, other, weights):
    count = len(own)
    side, rows, _ = own[0].shape
    width = hidden_width(weights)

    def kernel(head_ref, *refs):
        own_refs, other_refs = refs[:count], refs[count : 2 * count]
        refs, outs = refs[2 * count : -2 * count], refs[-2 * count :]
        for e in range(count):
            mine = to_hidden(flat(own_refs[e]), refs, e, head_ref[0])
            outs[2 * e][...] = mine.reshape(side, rows, width)
            theirs = to_hidden(flat(other_refs[e]), refs, e, 1 - head_ref[0])
            outs[2 * e + 1][...] = theirs.reshape(side, rows, width)

    shape = jax.ShapeDtypeStruct((side, rows, width), F32)
    made = call(kernel, [shape] * (2 * count), *own, *other, *weights, head=head)
    return [made[2 * e : 2 * e + 2] for e in range(count)]


def sum_hidden(half, own_refs, other_refs, refs, out_ref, e, start):
    side, rows = out_ref.shape[0], out_ref.shape[2]
    for b in range(side):
        if start is not None and b == 0:
            out_ref[0] = start[0][...]
        else:
            made = to_hidden(flat(own_refs[b]), refs, e, half)
            out_ref[b] = made.reshape(side, rows, made.shape[1])
    for a in range(side):
        if start is not None and a == 0:
            made = flat(start[1])
        else:
            made = to_hidden(flat(other_refs[a]), refs, e, 1 - half)
        for b in range(side):
            out_ref[b, a] += made[b * rows : (b + 1) * rows]


def whole_hidden(head, own, other, weights):
    side = len(own)
    count, _, rows, _ = own[0].shape

    def kernel(head_ref, *refs):
        weight_refs, out_ref = refs[2 * side : -1], refs[-1]
        for e in range(count):
            own_refs = [ref.at[e] for ref in refs[:side]]
            other_refs = [ref.at[e] for ref in refs[side : 2 * side]]
            sum_hidden(
                head_ref[0], own_refs, other_refs, weight_refs, out_ref.at[e], e, None
            )

    shape = jax.ShapeDtypeStruct((count, side, side, rows, hidden_width(weights)), F32)
    return call(kernel, shape, *own, *other, *weights, head=head)


def column(ref, a):
    side, rows, width = ref.shape[1:]
    return ref[a].reshape(side * rows, width)


def send_column(head_ref, rows_ref, refs, outs, e, k):
    made = from_hidden(column(rows_ref, k), refs, e, 1 - head_ref[0]).astype(BF)
    side, rows = rows_ref.shape[1:3]
    for b in range(side):
        outs[k * side + b][...] = made[b * rows : (b + 1) * rows]


def forward(head, e, own, other, start, weights, down):
    side = len(own) + 1
    _, rows, features = own[0].shape
    width = hidden_width(weights)
    half = width // 2

    def kernel(head_ref, *refs):
        refs = list(refs)
        own_refs = [None] + [refs.pop(0) for _ in range(side - 1)]
        other_refs = [None] + [refs.pop(0) for _ in range(side - 1)]
        begin = [refs.pop(0), refs.pop(0)]
        weight_refs = [refs.pop(0), refs.pop(0)]
        down_ref, hidden_ref, units_ref = refs[:3]
        sum_hidden(head_ref[0], own_refs, other_refs, weight_refs, hidden_ref, e, begin)
        for a in range(side):
            for b in range(side):
                gate = hidden_ref[b, a, :, :half]
                upper = hidden_ref[b, a, :, half:]
                silu = gate / (1.0 + jnp.exp(-gate))
                units_ref[a, b] = (silu * upper).astype(BF)
        for k in range(side - 1, -1, -1):
            send_column(head_ref, units_ref, [down_ref], refs[3:], e, k)

    shapes = [
        jax.ShapeDtypeStruct((side, side, rows, width), F32),
        jax.ShapeDtypeStruct((side, side, rows, half), BF),
    ] + [jax.ShapeDtypeStruct((rows, features), BF)] * (side * side)
    made = call(kernel, shapes, *own, *other, *start, *weights, down, head=head)
    return made[0], made[1], made[2:]


def backward(head, hidden, units_grad, weights):
    count = len(hidden)
    side, _, rows, width = hidden[0].shape
    half = width // 2
    features = weights[0].shape[1] // 2
    blocks = side * side

    def kernel(head_ref, *refs):
        hidden_refs, (grad_ref, gate_ref, up_ref) = refs[:count], refs[count : count + 3]
        outs = refs[count + 3 :]
        for e in range(count):
            both_ref, sends = outs[e], outs[count + e * blocks : count + (e + 1) * blocks]
            for a in range(side):
                for b in range(side):
                    gate = hidden_refs[e][b, a, :, :half]
                    upper = hidden_refs[e][b, a, :, half:]
                    grad = grad_ref[e, b, a]
                    sigmoid = 1.0 / (1.0 + jnp.exp(-gate))
                    slope = sigmoid * (1.0 + gate * (1.0 - sigmoid))
                    both_ref[a, b, :, :half] = (grad * upper * slope).astype(BF)
                    both_ref[a, b, :, half:] = (grad * (gate * sigmoid)).astype(BF)
            for k in range(side - 1, -1, -1):
                send_column(head_ref, both_ref, [gate_ref, up_ref], sends, e, k)

    shapes = [jax.ShapeDtypeStruct((side, side, rows, width), BF)] * count + [
        jax.ShapeDtypeStruct((rows, features), BF)
    ] * (count * blocks)
    made = call(kernel, shapes, *hidden, units_grad, *weights, head=head)
    sends = [made[count + e * blocks : count + (e + 1) * blocks] for e in range(count)]
    return made[:count], sends


def finish(head, rows, weights, arrived, k):
    count, side = len(rows), rows[0].shape[0]
    block, features = arrived[0][0].shape

    def kernel(head_ref, *refs):
        rows_refs, weight_refs = refs[:count], refs[count : -count * side - 1]
        arrived_refs, out_ref = refs[-count * side - 1 : -1], refs[-1]
        for e in range(count):
            mine = jnp.concatenate([rows_refs[e][a, k] for a in range(side)], axis=0)
            made = from_hidden(mine, weight_refs, e, head_ref[0])
            for a in range(side):
                added = arrived_refs[e * side + a][...].astype(F32)
                added = made[a * block : (a + 1) * block] + added
                out_ref[e, a] = added.astype(BF)

    shape = jax.ShapeDtypeStruct((count, side, block, features), BF)
    arrived = sum(map(list, arrived), [])
    return call(kernel, shape, *rows, *weights, *arrived, head=head)


def weight_grad(head, units, own, other):
    side = len(own)
    count, _, rows, features = own[0].shape
    width = units[0].shape[3]

    def kernel(head_ref, *refs):
        units_refs, refs, out_ref = refs[:count], refs[count:-1], refs[-1]
        dims = (((0,), (0,)), ((), ()))
        spot = pl.multiple_of(head_ref[0] * features, features)
        away = pl.multiple_of((1 - head_ref[0]) * features, features)
        for e in range(count):
            by_own = [units_refs[e][a, b] for b in range(side) for a in range(side)]
            by_other = [units_refs[e][a, b] for a in range(side) for b in range(side)]
            for order, refs_of, lane in (
                (by_own, refs[:side], spot),
                (by_other, refs[side:], away),
            ):
                left = jnp.concatenate(order, axis=0)
                right = jnp.concatenate([flat(ref, e) for ref in refs_of], axis=0)
                made = lax.dot_general(left, right, dims, preferred_element_type=F32)
                out_ref[e, :, pl.ds(lane, features)] = made.astype(BF)

    shape = jax.ShapeDtypeStruct((count, width, 2 * features), BF)
    return call(kernel, shape, *units, *own, *other, head=head)


def local(
    inputs,
    queries,
    keys,
    values,
    lengths,
    out_weight,
    norm_gain,
    expert_ids,
    gate_codes,
    gate_weight,
    up_weight,
    down_weight,
    cotangent,
):
    devices = lax.axis_size("ctx")
    position = lax.axis_index("ctx")
    head = lax.axis_index("head")
    deep, side = grid_of(devices)
    plane = side * side

    def swap(rows):
        return swap_cores(rows, devices)

    def z_masks(k):
        return (k * plane, k * plane)

    def a_masks(k):
        return (k, k * side)

    def b_masks(k):
        return (k * side, k)

    def along(array, masks_of, count):
        return [array] + [exchange(array, devices, masks_of(k)) for k in range(1, count)]

    local_tokens, local_heads, head_width = queries.shape
    kv_heads = keys.shape[1]
    head_groups = local_heads // kv_heads
    half_width = inputs.shape[1]
    capacity = max(2, 5 * TOK_DEV * TOP // (4 * EXP_DEV * devices))
    tokens = deep * local_tokens
    block_rows = -(-deep * capacity // 16) * 16

    joint = (gate_weight, up_weight)

    packed = jnp.concatenate(
        [
            keys.transpose(1, 0, 2).reshape(kv_heads * local_tokens, head_width),
            values.transpose(1, 0, 2).reshape(kv_heads * local_tokens, head_width),
            expert_ids.T.astype(BF),
            gate_codes.T.astype(BF),
        ],
        axis=0,
    )
    pack_z = jnp.stack(along(packed, z_masks, deep))
    pack_a = jnp.stack(along(pack_z, a_masks, side))
    pack_b = along(pack_a, b_masks, side)
    chunks = devices

    order = jnp.arange(chunks, dtype=jnp.int32)
    z_part, a_part, b_part = order % deep, order // deep % side, order // (deep * side)
    shift = jnp.where(head == 0, a_part + b_part * side, a_part * side + b_part)
    sources = position ^ (z_part * plane + shift)

    def places_of(owner):
        within = jnp.arange(local_tokens, dtype=jnp.int32)
        half = local_tokens // 2
        owner = owner[..., None]
        return jnp.where(
            within < half, owner * half + within, (2 * devices - 1 - owner) * half + within - half
        )

    docs_in = lengths.shape[0]
    upto = jnp.arange(docs_in)[:, None] <= jnp.arange(docs_in)[None, :]
    ends = jnp.sum(jnp.where(upto, lengths[:, None], 0), axis=0)
    high = places_of(position[None])[0][:, None]
    low = jnp.max(jnp.where(high >= ends[None, :], ends[None, :], 0), axis=1, keepdims=True)
    key_places = places_of(sources).reshape(side, 1, side * deep * local_tokens)
    grouped = queries.transpose(1, 0, 2)
    carry = None
    for k in range(side - 1):
        part = pack_b[k].reshape(side * deep, *packed.shape)
        carry = attend(carry, head_groups, grouped, part, key_places[k], low, high)
    part = pack_b[-1].reshape(side * deep, *packed.shape)
    made, made_bf = attend_and_project(
        head,
        inputs,
        swap(inputs),
        carry,
        head_groups,
        grouped,
        part,
        key_places[-1],
        low,
        high,
        out_weight,
    )

    upstream = cotangent.astype(F32)
    cot_z = along(after(cotangent, pack_z), z_masks, deep)
    cot_z = jnp.stack(after(tuple(cot_z), made_bf)).reshape(tokens, half_width)
    cot_a = along(cot_z, a_masks, side)

    arrived = swap(made_bf)
    normed, stream, inverse = normalize(head, made, arrived, norm_gain.reshape(1, half_width))
    wide = stream.astype(F32)
    gain = norm_gain.astype(F32)

    near = pack_a[..., -2 * TOP :, :].astype(jnp.int32)
    near_ids, near_codes = near[..., :TOP, :], near[..., TOP:, :].astype(F32)
    near_total = jnp.sum(near_codes, axis=-2)
    owners = position ^ (jnp.arange(side, dtype=jnp.int32) * jnp.where(head == 0, side, 1))
    experts = owners[:, None] * EXP_DEV + jnp.arange(EXP_DEV, dtype=jnp.int32)
    hit = near_ids == experts[:, :, None, None, None, None]
    share = jnp.sum(jnp.where(hit, near_codes, 0.0), axis=-2) / near_total
    member = jnp.any(hit, axis=-2)
    before = jnp.arange(local_tokens)[:, None] < jnp.arange(local_tokens)[None, :]
    rank = jnp.einsum(
        "keazt,tu->keazu", member.astype(BF), before.astype(BF), preferred_element_type=F32
    ).astype(jnp.int32)
    slot = jnp.arange(deep, dtype=jnp.int32)[:, None] * capacity + rank
    slot = jnp.where(member, slot, -1)
    slot = slot.reshape(side, EXP_DEV, side, tokens)
    share = share.reshape(side, EXP_DEV, side, tokens)
    hot = slot[..., None, :] == jnp.arange(block_rows, dtype=jnp.int32)[:, None]
    hot_share = jnp.where(hot, share[..., None, :], 0.0).astype(BF)
    hot = hot.astype(BF)

    experts_here = range(EXP_DEV)

    def to_b(rows):
        return [exchange(rows[k], devices, b_masks(k)) for k in range(1, side)]

    def dense(matrix, got, a, lanes):
        out = 0.0
        for e in experts_here:
            for k in range(side):
                out = out + jnp.einsum(
                    "ru,rd->ud", matrix[k, e, a, :, lanes], got[e][k][a], preferred_element_type=F32
                )
        return out

    def return_pieces(matrix, got, step, waits):
        arrived, near_sum, across, passed = [], None, [], []
        for first in range(deep - step, -1, -step):
            lanes = slice(first * local_tokens, (first + step) * local_tokens)
            late = (waits, arrived[:1]) if first < deep - 2 * step else ()
            each = []
            for a in range(1, side):
                rows = after(dense(matrix, got, a, lanes).astype(BF), late)
                each.append(exchange(rows, devices, a_masks(a)))
            arrived += each
            level = dense(matrix, got, 0, lanes)
            for rows in after(tuple(each), level):
                level = level + rows.astype(F32)
            for z in range(first + step - 1, first - 1, -1):
                near_sum = level[(z - first) * local_tokens : (z - first + 1) * local_tokens]
                if z > 0:
                    passed.append(near_sum.astype(BF))
                    across.append(exchange(passed[-1], devices, z_masks(z)))
        return arrived, near_sum, across

    def last_sum(near_sum, across):
        for rows in across:
            near_sum = near_sum + rows.astype(F32)
        return near_sum

    norm_z = along(normed, z_masks, deep)
    cot_a = list(after(tuple(cot_a), normed))
    cot_out = [dispatch(hot_share[k], cot_a, False) for k in range(side)]
    incoming = [cot_out[0]] + to_b(cot_out)
    incoming_other = [swap(rows) for rows in incoming]
    norm_z = jnp.stack(after(tuple(norm_z), *cot_out)).reshape(tokens, half_width)
    norm_a = along(norm_z, a_masks, side)
    norm_out = [None] + [dispatch(hot[k], norm_a, False) for k in range(1, side)]
    norm_b = to_b(norm_out)
    norm_out[0] = dispatch(after(hot[0], norm_out[1:]), norm_a, True)
    units_grad = whole_hidden(head, incoming, incoming_other, (down_weight,))
    start = half_hidden(head, norm_out[0], [swap(rows) for rows in norm_out[0]], joint)
    norm_b = after(tuple(norm_b), (start, units_grad))

    hidden, units, theirs = [], [], []
    own_rows = [[rows[e] for rows in norm_b] for e in experts_here]
    other_rows = [[swap(rows) for rows in each] for each in own_rows]
    for e in experts_here:
        other = list(after(tuple(other_rows[e]), units))
        made = forward(head, e, own_rows[e], other, start[e], joint, down_weight)
        hidden.append(made[0])
        units.append(made[1])
        theirs.append(made[2])

    def finish_all(rows, weights, theirs):
        done = [None] * side
        for k in range(side - 1, -1, -1):
            arrived = [
                [swap(part) for part in each[k * side : (k + 1) * side]] for each in theirs
            ]
            done[k] = finish(head, rows, weights, arrived, k)
        return done

    total = finish_all(units, (down_weight,), theirs)
    sent = to_b(total)
    both, theirs = backward(head, list(after(tuple(hidden), total)), units_grad, joint)
    back_total = finish_all(both, joint, theirs)
    sent = after(tuple(sent), both)
    total = [total[0]] + list(sent)
    got = [[rows[e] for rows in total] for e in experts_here]
    arrived, near_sum, across = return_pieces(hot_share, got, deep, ())
    back_total = [back_total[0]] + to_b([None] + list(after(tuple(back_total[1:]), arrived)))
    got = [[rows[e] for rows in back_total] for e in experts_here]
    arrived, back_sum, back_across = return_pieces(hot, got, 2, across)
    output = (wide + last_sum(near_sum, across)).astype(BF)
    down_grad = weight_grad(head, after(tuple(units), arrived), incoming, incoming_other)
    scaled = last_sum(back_sum, after(tuple(back_across), (down_grad, output))) * gain
    inner = jnp.sum(scaled * wide, axis=1, keepdims=True)
    inner = inner + swap(inner)
    input_grad = (upstream + inverse * scaled - wide * inverse**3 * inner / D).astype(BF)
    norm_term = (inverse**2 * inner / D**0.5)[:, 0]
    return (output, input_grad, down_grad, norm_term)


def solution(mesh):
    in_specs = (
        P("ctx", "head"),
        P("ctx", "head", None),
        P("ctx", "head", None),
        P("ctx", "head", None),
        P(),
        P("head", None),
        P("head"),
        P("ctx", None),
        P("ctx", None),
        P("ctx", None, "head"),
        P("ctx", None, "head"),
        P("ctx", "head", None),
        P("ctx", "head"),
    )
    out_specs = (P("ctx", "head"), P("ctx", "head"), P("ctx", "head", None), P("ctx"))
    return jax.shard_map(local, mesh=mesh, in_specs=in_specs, out_specs=out_specs, check_vma=False)
```

```python
import jax
import jax.numpy as jnp
from jax import lax
from jax.experimental import pallas as pl
from jax.experimental.pallas import tpu as pltpu
from jax.sharding import PartitionSpec as P

D = 2048
TOP = 8
EXP_DEV = 2
TOK_DEV = 128
BF = jnp.bfloat16
F32 = jnp.float32
AXES = ("ctx", "head")
CHEAP = pl.CostEstimate(flops=1, bytes_accessed=1, transcendentals=0)


def grid_of(devices):
    side = 2 if devices < 64 else 4
    return devices // (side * side), side


def exchange(array, devices, masks):
    pairs = [
        (c * 2 + h, (c ^ masks[h]) * 2 + h) for c in range(devices) for h in range(2)
    ]
    return lax.ppermute(array, AXES, pairs)


def swap_cores(array, devices):
    pairs = [(c * 2 + h, c * 2 + 1 - h) for c in range(devices) for h in range(2)]
    return lax.ppermute(array, AXES, pairs)


LOG2E = 1.4426950408889634


def after(value, *others):
    return lax.optimization_barrier((value, others))[0]


def attend_heads(head_groups, q_ref, kv_ref, place_ref, low_ref, high_ref, bias_ref, made_ref):
    heads, tokens, width = q_ref.shape
    chunks = kv_ref.shape[0]
    count = chunks * tokens
    kv_heads = heads // head_groups
    place = place_ref[...]
    seen = (place >= low_ref[...]) & (place <= high_ref[...])
    bias_ref[...] = jnp.where(seen, 0.0, -1e30)
    factor = width ** (-0.5) * LOG2E
    for kv in range(kv_heads):
        key = kv_ref[:, kv * tokens : (kv + 1) * tokens, :].reshape(count, width)
        start = (kv_heads + kv) * tokens
        value = kv_ref[:, start : start + tokens, :].reshape(count, width)
        for group in range(head_groups):
            head = kv * head_groups + group
            scores = lax.dot_general(
                q_ref[head], key, (((1,), (1,)), ((), ())), preferred_element_type=F32
            )
            scores = scores + bias_ref[...]
            top = jnp.max(scores, axis=1, keepdims=True)
            weights = jnp.exp2((scores - top) * factor)
            total = jnp.sum(weights, axis=1, keepdims=True)
            mixed = jnp.dot(weights.astype(BF), value, preferred_element_type=F32)
            made_ref[head, :, :width] = jnp.broadcast_to(top, (tokens, width))
            made_ref[head, :, width : 2 * width] = jnp.broadcast_to(total, (tokens, width))
            made_ref[head, :, 2 * width :] = mixed


def merge_heads(first_ref, second_ref, head, width):
    factor = width ** (-0.5) * LOG2E
    parts = []
    for ref in (first_ref, second_ref):
        parts.append([ref[head, :, n * width : (n + 1) * width] for n in range(3)])
    top = jnp.maximum(parts[0][0], parts[1][0])
    keep = [jnp.exp2((part[0] - top) * factor) for part in parts]
    total = parts[0][1] * keep[0] + parts[1][1] * keep[1]
    mixed = parts[0][2] * keep[0] + parts[1][2] * keep[1]
    return top, total, mixed


def attend(carry, head_groups, q, kv, place, low, high):
    heads, tokens, width = q.shape
    count = kv.shape[0] * tokens
    wide = 3 * width
    first = carry is None

    def kernel(*refs):
        out_ref, bias_ref, made_ref, held_ref, sems, held_sem = refs[-6:]
        if not first:
            held_copy = pltpu.make_async_copy(refs[5], held_ref, held_sem)
            held_copy.start()
        attend_heads(head_groups, *refs[:5], bias_ref, made_ref)
        if not first:
            held_copy.wait()
            for head in range(heads):
                merged = merge_heads(held_ref, made_ref, head, width)
                for n in range(3):
                    made_ref[head, :, n * width : (n + 1) * width] = merged[n]
        copy = pltpu.make_async_copy(made_ref, out_ref, sems)
        copy.start()
        copy.wait()

    vmem, far = pl.BlockSpec(memory_space=pltpu.VMEM), pl.BlockSpec(memory_space=pltpu.HBM)
    carry_shape = (heads, tokens, wide)
    return pl.pallas_call(
        kernel,
        out_shape=jax.ShapeDtypeStruct(carry_shape, F32),
        in_specs=[vmem] * 5 + ([] if first else [far]),
        out_specs=far,
        scratch_shapes=[
            pltpu.VMEM((tokens, count), F32),
            pltpu.VMEM(carry_shape, F32),
            pltpu.VMEM((8, 128) if first else carry_shape, F32),
            pltpu.SemaphoreType.DMA,
            pltpu.SemaphoreType.DMA,
        ],
        compiler_params=pltpu.CompilerParams(vmem_limit_bytes=(18 << 20) + 5 * tokens * count * 4),
        cost_estimate=CHEAP,
    )(q, kv, place, low, high, *(() if first else (carry,)))


def attend_and_project(
    half, inputs, other_inputs, carry, head_groups, q, kv, place, low, high, weight
):
    heads, tokens, width = q.shape
    count = kv.shape[0] * tokens
    features = weight.shape[1]
    pieces = 4
    rows = weight.shape[0] // pieces

    def kernel(*refs):
        half_ref, refs = refs[0], refs[1:]
        carry_ref, weight_ref, in_ref, other_ref, out_ref, send_ref = refs[5:11]
        bias_ref, held, made_ref, weight_held, heads_ref, in_held, held_sem, weight_sems, in_sems = (
            refs[11:]
        )
        held_copy = pltpu.make_async_copy(carry_ref, held, held_sem)
        held_copy.start()
        in_copies = [
            pltpu.make_async_copy(ref, in_held.at[n], in_sems.at[n])
            for n, ref in enumerate((in_ref, other_ref))
        ]
        for copy in in_copies:
            copy.start()
        copies = []
        for n in range(pieces):
            at = pl.ds(n * rows, rows)
            copies.append(
                pltpu.make_async_copy(weight_ref.at[at], weight_held.at[at], weight_sems.at[n])
            )
            copies[n].start()
        attend_heads(head_groups, *refs[:5], bias_ref, made_ref)
        held_copy.wait()
        for head in range(heads):
            _, total, mixed = merge_heads(held, made_ref, head, width)
            heads_ref[:, head * width : (head + 1) * width] = (mixed / total).astype(BF)
        for copy in copies:
            copy.wait()
        step = 512
        for at in range(0, features, step):
            made = contract(heads_ref[...], weight_held[:, at : at + step], False)
            out_ref[:, at : at + step] = made
            send_ref[:, at : at + step] = made.astype(BF)
        own = in_ref.shape[1]
        for n, copy in enumerate(in_copies):
            copy.wait()
            side_of = half_ref[0] if n == 0 else 1 - half_ref[0]
            lanes = pl.ds(pl.multiple_of(side_of * own, own), own)
            out_ref[:, lanes] += in_held[n].astype(F32)

    vmem, far = pl.BlockSpec(memory_space=pltpu.VMEM), pl.BlockSpec(memory_space=pltpu.HBM)
    return pl.pallas_call(
        kernel,
        out_shape=[jax.ShapeDtypeStruct((tokens, features), kind) for kind in (F32, BF)],
        in_specs=[pl.BlockSpec(memory_space=pltpu.SMEM)] + [vmem] * 5 + [far] * 4,
        out_specs=[vmem, vmem],
        scratch_shapes=[
            pltpu.VMEM((tokens, count), F32),
            pltpu.VMEM(carry.shape, F32),
            pltpu.VMEM(carry.shape, F32),
            pltpu.VMEM(weight.shape, BF),
            pltpu.VMEM((tokens, heads * width), BF),
            pltpu.VMEM((2, *inputs.shape), BF),
            pltpu.SemaphoreType.DMA,
            pltpu.SemaphoreType.DMA((pieces,)),
            pltpu.SemaphoreType.DMA((2,)),
        ],
        compiler_params=pltpu.CompilerParams(vmem_limit_bytes=58 << 20),
        cost_estimate=CHEAP,
    )(half.reshape(1), q, kv, place, low, high, carry, weight, inputs, other_inputs)


def call(kernel, out_shape, *operands, head=None):
    size = sum(x.size * x.dtype.itemsize for x in jax.tree.leaves((operands, out_shape)))
    vmem = pl.BlockSpec(memory_space=pltpu.VMEM)
    in_specs = [vmem] * len(operands)
    if head is not None:
        in_specs = [pl.BlockSpec(memory_space=pltpu.SMEM)] + in_specs
        operands = (head.reshape(1), *operands)
    return pl.pallas_call(
        kernel,
        out_shape=out_shape,
        in_specs=in_specs,
        out_specs=jax.tree.map(lambda _: vmem, out_shape),
        compiler_params=pltpu.CompilerParams(vmem_limit_bytes=size + 6 * 1024 * 1024),
        cost_estimate=CHEAP,
    )(*operands)


def contract(rows, weight, flipped):
    dims = (((1,), (1 if flipped else 0,)), ((), ()))
    return lax.dot_general(rows, weight, dims, preferred_element_type=F32)


def flat(ref, expert=None):
    blocks, rows, width = ref.shape[-3:]
    return (ref[...] if expert is None else ref[expert]).reshape(blocks * rows, width)


def features_of(half, refs):
    count = refs[0].shape[1 if len(refs) == 2 else 2] // 2
    return pl.ds(pl.multiple_of(half * count, count), count)


def to_hidden(rows, refs, e, half):
    spot = features_of(half, refs)
    if len(refs) == 2:
        made = [contract(rows, ref[e, spot, :], False) for ref in refs]
        return jnp.concatenate(made, axis=1)
    return contract(rows, refs[0][e, :, spot], True)


def from_hidden(rows, refs, e, half):
    spot = features_of(half, refs)
    if len(refs) == 2:
        width = refs[0].shape[2]
        made = [
            contract(rows[:, n * width : (n + 1) * width], refs[n][e, spot, :], True)
            for n in range(2)
        ]
        return made[0] + made[1]
    return contract(rows, refs[0][e, :, spot], False)


def hidden_width(weights):
    return weights[0].shape[2] * 2 if len(weights) == 2 else weights[0].shape[1]


def dispatch(matrix, level, apart):
    count, side, rows, _ = matrix.shape
    width = level[0].shape[1]

    def kernel(matrix_ref, *refs):
        level_refs, outs = refs[:side], refs[side:]
        for e in range(count):
            out_ref = outs[e] if apart else outs[0].at[e]
            for a in range(side):
                out_ref[a] = contract(matrix_ref[e, a], level_refs[a][...], False).astype(BF)

    if apart:
        shapes = [jax.ShapeDtypeStruct((side, rows, width), BF)] * count
    else:
        shapes = [jax.ShapeDtypeStruct((count, side, rows, width), BF)]
    made = call(kernel, shapes, matrix, *level)
    return made if apart else made[0]


def normalize(head, made, arrived, gain):
    rows, width = made.shape[0], gain.shape[1]

    def kernel(head_ref, made_ref, arrived_ref, gain_ref, *outs):
        def stream_of(half):
            lanes = pl.ds(pl.multiple_of(half * width, width), width)
            return (made_ref[:, lanes] + arrived_ref[:, lanes].astype(F32)).astype(BF)

        stream = stream_of(head_ref[0])
        wide = stream.astype(F32)
        other = stream_of(1 - head_ref[0]).astype(F32)
        squares = jnp.sum(wide * wide + other * other, axis=1, keepdims=True)
        inverse = lax.rsqrt(squares / D + 1e-06)
        outs[0][...] = (wide * inverse * gain_ref[...].astype(F32)).astype(BF)
        outs[1][...] = stream
        outs[2][...] = inverse

    shapes = [
        jax.ShapeDtypeStruct((rows, width), BF),
        jax.ShapeDtypeStruct((rows, width), BF),
        jax.ShapeDtypeStruct((rows, 1), F32),
    ]
    return call(kernel, shapes, made, arrived, gain, head=head)


def half_hidden(head, own, other, weights):
    count = len(own)
    side, rows, _ = own[0].shape
    width = hidden_width(weights)

    def kernel(head_ref, *refs):
        own_refs, other_refs = refs[:count], refs[count : 2 * count]
        refs, outs = refs[2 * count : -2 * count], refs[-2 * count :]
        for e in range(count):
            mine = to_hidden(flat(own_refs[e]), refs, e, head_ref[0])
            outs[2 * e][...] = mine.reshape(side, rows, width)
            theirs = to_hidden(flat(other_refs[e]), refs, e, 1 - head_ref[0])
            outs[2 * e + 1][...] = theirs.reshape(side, rows, width)

    shape = jax.ShapeDtypeStruct((side, rows, width), F32)
    made = call(kernel, [shape] * (2 * count), *own, *other, *weights, head=head)
    return [made[2 * e : 2 * e + 2] for e in range(count)]


def sum_hidden(half, own_refs, other_refs, refs, out_ref, e, start):
    side, rows = out_ref.shape[0], out_ref.shape[2]
    for b in range(side):
        if start is not None and b == 0:
            out_ref[0] = start[0][...]
        else:
            made = to_hidden(flat(own_refs[b]), refs, e, half)
            out_ref[b] = made.reshape(side, rows, made.shape[1])
    for a in range(side):
        if start is not None and a == 0:
            made = flat(start[1])
        else:
            made = to_hidden(flat(other_refs[a]), refs, e, 1 - half)
        for b in range(side):
            out_ref[b, a] += made[b * rows : (b + 1) * rows]


def whole_hidden(head, own, other, weights):
    side = len(own)
    count, _, rows, _ = own[0].shape

    def kernel(head_ref, *refs):
        weight_refs, out_ref = refs[2 * side : -1], refs[-1]
        for e in range(count):
            own_refs = [ref.at[e] for ref in refs[:side]]
            other_refs = [ref.at[e] for ref in refs[side : 2 * side]]
            sum_hidden(
                head_ref[0], own_refs, other_refs, weight_refs, out_ref.at[e], e, None
            )

    shape = jax.ShapeDtypeStruct((count, side, side, rows, hidden_width(weights)), F32)
    return call(kernel, shape, *own, *other, *weights, head=head)


def column(ref, a):
    side, rows, width = ref.shape[1:]
    return ref[a].reshape(side * rows, width)


def send_column(head_ref, rows_ref, refs, outs, e, k):
    made = from_hidden(column(rows_ref, k), refs, e, 1 - head_ref[0])
    outs[k][...] = made.astype(BF).reshape(outs[k].shape)


def forward(head, e, own, other, start, weights, down):
    side = len(own) + 1
    _, rows, features = own[0].shape
    width = hidden_width(weights)
    half = width // 2

    def kernel(head_ref, *refs):
        refs = list(refs)
        own_refs = [None] + [refs.pop(0) for _ in range(side - 1)]
        other_refs = [None] + [refs.pop(0) for _ in range(side - 1)]
        begin = [refs.pop(0), refs.pop(0)]
        weight_refs = [refs.pop(0), refs.pop(0)]
        down_ref, hidden_ref, units_ref = refs[:3]
        sum_hidden(head_ref[0], own_refs, other_refs, weight_refs, hidden_ref, e, begin)
        for a in range(side):
            for b in range(side):
                gate = hidden_ref[b, a, :, :half]
                upper = hidden_ref[b, a, :, half:]
                silu = gate / (1.0 + jnp.exp(-gate))
                units_ref[a, b] = (silu * upper).astype(BF)
        for k in range(side - 1, -1, -1):
            send_column(head_ref, units_ref, [down_ref], refs[3:], e, k)

    shapes = [
        jax.ShapeDtypeStruct((side, side, rows, width), F32),
        jax.ShapeDtypeStruct((side, side, rows, half), BF),
    ] + [jax.ShapeDtypeStruct((side, rows, features), BF)] * side
    made = call(kernel, shapes, *own, *other, *start, *weights, down, head=head)
    return made[0], made[1], made[2:]


def backward(head, hidden, units_grad, weights):
    count = len(hidden)
    side, _, rows, width = hidden[0].shape
    half = width // 2
    features = weights[0].shape[1] // 2
    blocks = side

    def kernel(head_ref, *refs):
        hidden_refs, (grad_ref, gate_ref, up_ref) = refs[:count], refs[count : count + 3]
        outs = refs[count + 3 :]
        for e in range(count):
            both_ref, sends = outs[e], outs[count + e * blocks : count + (e + 1) * blocks]
            for a in range(side):
                for b in range(side):
                    gate = hidden_refs[e][b, a, :, :half]
                    upper = hidden_refs[e][b, a, :, half:]
                    grad = grad_ref[e, b, a]
                    sigmoid = 1.0 / (1.0 + jnp.exp(-gate))
                    slope = sigmoid * (1.0 + gate * (1.0 - sigmoid))
                    both_ref[a, b, :, :half] = (grad * upper * slope).astype(BF)
                    both_ref[a, b, :, half:] = (grad * (gate * sigmoid)).astype(BF)
            for k in range(side - 1, -1, -1):
                send_column(head_ref, both_ref, [gate_ref, up_ref], sends, e, k)

    shapes = [jax.ShapeDtypeStruct((side, side, rows, width), BF)] * count + [
        jax.ShapeDtypeStruct((side, rows, features), BF)
    ] * (count * blocks)
    made = call(kernel, shapes, *hidden, units_grad, *weights, head=head)
    sends = [made[count + e * blocks : count + (e + 1) * blocks] for e in range(count)]
    return made[:count], sends


def finish(head, rows, weights, arrived, k):
    count = len(rows)
    side, block, features = arrived[0].shape

    def kernel(head_ref, *refs):
        rows_refs, weight_refs = refs[:count], refs[count : -count - 1]
        arrived_refs, out_ref = refs[-count - 1 : -1], refs[-1]
        for e in range(count):
            mine = jnp.concatenate([rows_refs[e][a, k] for a in range(side)], axis=0)
            made = from_hidden(mine, weight_refs, e, head_ref[0])
            for a in range(side):
                added = arrived_refs[e][a].astype(F32)
                added = made[a * block : (a + 1) * block] + added
                out_ref[e, a] = added.astype(BF)

    shape = jax.ShapeDtypeStruct((count, side, block, features), BF)
    return call(kernel, shape, *rows, *weights, *arrived, head=head)


def weight_grad(head, units, own, other):
    side = len(own)
    count, _, rows, features = own[0].shape
    width = units[0].shape[3]

    def kernel(head_ref, *refs):
        units_refs, refs, out_ref = refs[:count], refs[count:-1], refs[-1]
        dims = (((0,), (0,)), ((), ()))
        spot = pl.multiple_of(head_ref[0] * features, features)
        away = pl.multiple_of((1 - head_ref[0]) * features, features)
        for e in range(count):
            by_own = [units_refs[e][a, b] for b in range(side) for a in range(side)]
            by_other = [units_refs[e][a, b] for a in range(side) for b in range(side)]
            for order, refs_of, lane in (
                (by_own, refs[:side], spot),
                (by_other, refs[side:], away),
            ):
                left = jnp.concatenate(order, axis=0)
                right = jnp.concatenate([flat(ref, e) for ref in refs_of], axis=0)
                made = lax.dot_general(left, right, dims, preferred_element_type=F32)
                out_ref[e, :, pl.ds(lane, features)] = made.astype(BF)

    shape = jax.ShapeDtypeStruct((count, width, 2 * features), BF)
    return call(kernel, shape, *units, *own, *other, head=head)


def local(
    inputs,
    queries,
    keys,
    values,
    lengths,
    out_weight,
    norm_gain,
    expert_ids,
    gate_codes,
    gate_weight,
    up_weight,
    down_weight,
    cotangent,
):
    devices = lax.axis_size("ctx")
    position = lax.axis_index("ctx")
    head = lax.axis_index("head")
    deep, side = grid_of(devices)
    plane = side * side

    def swap(rows):
        return swap_cores(rows, devices)

    def z_masks(k):
        return (k * plane, k * plane)

    def a_masks(k):
        return (k, k * side)

    def b_masks(k):
        return (k * side, k)

    def along(array, masks_of, count):
        return [array] + [exchange(array, devices, masks_of(k)) for k in range(1, count)]

    local_tokens, local_heads, head_width = queries.shape
    kv_heads = keys.shape[1]
    head_groups = local_heads // kv_heads
    half_width = inputs.shape[1]
    capacity = max(2, 5 * TOK_DEV * TOP // (4 * EXP_DEV * devices))
    tokens = deep * local_tokens
    block_rows = -(-deep * capacity // 16) * 16

    joint = (gate_weight, up_weight)

    packed = jnp.concatenate(
        [
            keys.transpose(1, 0, 2).reshape(kv_heads * local_tokens, head_width),
            values.transpose(1, 0, 2).reshape(kv_heads * local_tokens, head_width),
            expert_ids.T.astype(BF),
            gate_codes.T.astype(BF),
        ],
        axis=0,
    )
    pack_z = jnp.stack(along(packed, z_masks, deep))
    pack_a = jnp.stack(along(pack_z, a_masks, side))
    pack_b = along(pack_a, b_masks, side)
    chunks = devices

    order = jnp.arange(chunks, dtype=jnp.int32)
    z_part, a_part, b_part = order % deep, order // deep % side, order // (deep * side)
    shift = jnp.where(head == 0, a_part + b_part * side, a_part * side + b_part)
    sources = position ^ (z_part * plane + shift)

    def places_of(owner):
        within = jnp.arange(local_tokens, dtype=jnp.int32)
        half = local_tokens // 2
        owner = owner[..., None]
        return jnp.where(
            within < half, owner * half + within, (2 * devices - 1 - owner) * half + within - half
        )

    docs_in = lengths.shape[0]
    upto = jnp.arange(docs_in)[:, None] <= jnp.arange(docs_in)[None, :]
    ends = jnp.sum(jnp.where(upto, lengths[:, None], 0), axis=0)
    high = places_of(position[None])[0][:, None]
    low = jnp.max(jnp.where(high >= ends[None, :], ends[None, :], 0), axis=1, keepdims=True)
    key_places = places_of(sources).reshape(side, 1, side * deep * local_tokens)
    grouped = queries.transpose(1, 0, 2)
    carry = None
    for k in range(side - 1):
        part = pack_b[k].reshape(side * deep, *packed.shape)
        carry = attend(carry, head_groups, grouped, part, key_places[k], low, high)
    part = pack_b[-1].reshape(side * deep, *packed.shape)
    made, made_bf = attend_and_project(
        head,
        inputs,
        swap(inputs),
        carry,
        head_groups,
        grouped,
        part,
        key_places[-1],
        low,
        high,
        out_weight,
    )

    upstream = cotangent.astype(F32)
    cot_z = along(after(cotangent, pack_z), z_masks, deep)
    cot_z = jnp.stack(after(tuple(cot_z), made_bf)).reshape(tokens, half_width)
    cot_a = along(cot_z, a_masks, side)

    arrived = swap(made_bf)
    normed, stream, inverse = normalize(head, made, arrived, norm_gain.reshape(1, half_width))
    wide = stream.astype(F32)
    gain = norm_gain.astype(F32)

    near = pack_a[..., -2 * TOP :, :].astype(jnp.int32)
    near_ids, near_codes = near[..., :TOP, :], near[..., TOP:, :].astype(F32)
    near_total = jnp.sum(near_codes, axis=-2)
    owners = position ^ (jnp.arange(side, dtype=jnp.int32) * jnp.where(head == 0, side, 1))
    experts = owners[:, None] * EXP_DEV + jnp.arange(EXP_DEV, dtype=jnp.int32)
    hit = near_ids == experts[:, :, None, None, None, None]
    share = jnp.sum(jnp.where(hit, near_codes, 0.0), axis=-2) / near_total
    member = jnp.any(hit, axis=-2)
    before = jnp.arange(local_tokens)[:, None] < jnp.arange(local_tokens)[None, :]
    rank = jnp.einsum(
        "keazt,tu->keazu", member.astype(BF), before.astype(BF), preferred_element_type=F32
    ).astype(jnp.int32)
    slot = jnp.arange(deep, dtype=jnp.int32)[:, None] * capacity + rank
    slot = jnp.where(member, slot, -1)
    slot = slot.reshape(side, EXP_DEV, side, tokens)
    share = share.reshape(side, EXP_DEV, side, tokens)
    hot = slot[..., None, :] == jnp.arange(block_rows, dtype=jnp.int32)[:, None]
    hot_share = jnp.where(hot, share[..., None, :], 0.0).astype(BF)
    hot = hot.astype(BF)

    experts_here = range(EXP_DEV)

    def to_b(rows):
        return [exchange(rows[k], devices, b_masks(k)) for k in range(1, side)]

    def dense(matrix, got, a, lanes):
        out = 0.0
        for e in experts_here:
            for k in range(side):
                out = out + jnp.einsum(
                    "ru,rd->ud", matrix[k, e, a, :, lanes], got[e][k][a], preferred_element_type=F32
                )
        return out

    def return_pieces(matrix, got, step, waits):
        arrived, near_sum, across, passed = [], None, [], []
        for first in range(deep - step, -1, -step):
            lanes = slice(first * local_tokens, (first + step) * local_tokens)
            late = (waits, arrived[:1]) if first < deep - 2 * step else ()
            each = []
            for a in range(1, side):
                rows = after(dense(matrix, got, a, lanes).astype(BF), late)
                each.append(exchange(rows, devices, a_masks(a)))
            arrived += each
            level = dense(matrix, got, 0, lanes)
            for rows in after(tuple(each), level):
                level = level + rows.astype(F32)
            for z in range(first + step - 1, first - 1, -1):
                near_sum = level[(z - first) * local_tokens : (z - first + 1) * local_tokens]
                if z > 0:
                    passed.append(near_sum.astype(BF))
                    across.append(exchange(passed[-1], devices, z_masks(z)))
        return arrived, near_sum, across

    def last_sum(near_sum, across):
        for rows in across:
            near_sum = near_sum + rows.astype(F32)
        return near_sum

    norm_z = along(normed, z_masks, deep)
    cot_a = list(after(tuple(cot_a), normed))
    cot_out = [dispatch(hot_share[k], cot_a, False) for k in range(side)]
    incoming = [cot_out[0]] + to_b(cot_out)
    incoming_other = [swap(rows) for rows in incoming]
    norm_z = jnp.stack(after(tuple(norm_z), *cot_out)).reshape(tokens, half_width)
    norm_a = along(norm_z, a_masks, side)
    norm_out = [None] + [dispatch(hot[k], norm_a, False) for k in range(1, side)]
    norm_b = to_b(norm_out)
    norm_out[0] = dispatch(after(hot[0], norm_out[1:]), norm_a, True)
    units_grad = whole_hidden(head, incoming, incoming_other, (down_weight,))
    start = half_hidden(head, norm_out[0], [swap(rows) for rows in norm_out[0]], joint)
    norm_b = after(tuple(norm_b), (start, units_grad))

    hidden, units, theirs = [], [], []
    own_rows = [[rows[e] for rows in norm_b] for e in experts_here]
    other_rows = [[swap(rows) for rows in each] for each in own_rows]
    for e in experts_here:
        other = list(after(tuple(other_rows[e]), units))
        made = forward(head, e, own_rows[e], other, start[e], joint, down_weight)
        hidden.append(made[0])
        units.append(made[1])
        theirs.append(made[2])

    def finish_all(rows, weights, theirs):
        done = [None] * side
        for k in range(side - 1, -1, -1):
            arrived = [swap(each[k]) for each in theirs]
            done[k] = finish(head, rows, weights, arrived, k)
        return done

    total = finish_all(units, (down_weight,), theirs)
    sent = to_b(total)
    both, theirs = backward(head, list(after(tuple(hidden), total)), units_grad, joint)
    back_total = finish_all(both, joint, theirs)
    sent = after(tuple(sent), both)
    total = [total[0]] + list(sent)
    got = [[rows[e] for rows in total] for e in experts_here]
    arrived, near_sum, across = return_pieces(hot_share, got, deep, ())
    back_total = [back_total[0]] + to_b([None] + list(after(tuple(back_total[1:]), arrived)))
    got = [[rows[e] for rows in back_total] for e in experts_here]
    arrived, back_sum, back_across = return_pieces(hot, got, 2, across)
    output = (wide + last_sum(near_sum, across)).astype(BF)
    down_grad = weight_grad(head, after(tuple(units), arrived), incoming, incoming_other)
    scaled = last_sum(back_sum, after(tuple(back_across[::-1]), (down_grad, output))) * gain
    inner = jnp.sum(scaled * wide, axis=1, keepdims=True)
    inner = inner + swap(inner)
    input_grad = (upstream + inverse * scaled - wide * inverse**3 * inner / D).astype(BF)
    norm_term = (inverse**2 * inner / D**0.5)[:, 0]
    return (output, input_grad, down_grad, norm_term)


def solution(mesh):
    in_specs = (
        P("ctx", "head"),
        P("ctx", "head", None),
        P("ctx", "head", None),
        P("ctx", "head", None),
        P(),
        P("head", None),
        P("head"),
        P("ctx", None),
        P("ctx", None),
        P("ctx", None, "head"),
        P("ctx", None, "head"),
        P("ctx", "head", None),
        P("ctx", "head"),
    )
    out_specs = (P("ctx", "head"), P("ctx", "head"), P("ctx", "head", None), P("ctx"))
    return jax.shard_map(local, mesh=mesh, in_specs=in_specs, out_specs=out_specs, check_vma=False)
```

```python
import jax
import jax.numpy as jnp
from jax import lax
from jax.experimental import pallas as pl
from jax.experimental.pallas import tpu as pltpu
from jax.sharding import PartitionSpec as P

D = 2048
TOP = 8
EXP_DEV = 2
TOK_DEV = 128
BF = jnp.bfloat16
F32 = jnp.float32
AXES = ("ctx", "head")
CHEAP = pl.CostEstimate(flops=1, bytes_accessed=1, transcendentals=0)


def grid_of(devices):
    side = 2 if devices < 64 else 4
    return devices // (side * side), side


def exchange(array, devices, masks):
    pairs = [
        (c * 2 + h, (c ^ masks[h]) * 2 + h) for c in range(devices) for h in range(2)
    ]
    return lax.ppermute(array, AXES, pairs)


def swap_cores(array, devices):
    pairs = [(c * 2 + h, c * 2 + 1 - h) for c in range(devices) for h in range(2)]
    return lax.ppermute(array, AXES, pairs)


LOG2E = 1.4426950408889634


def after(value, *others):
    return lax.optimization_barrier((value, others))[0]


def attend_heads(head_groups, q_ref, kv_ref, place_ref, low_ref, high_ref, bias_ref, made_ref):
    heads, tokens, width = q_ref.shape
    chunks = kv_ref.shape[0]
    count = chunks * tokens
    kv_heads = heads // head_groups
    place = place_ref[...]
    seen = (place >= low_ref[...]) & (place <= high_ref[...])
    bias_ref[...] = jnp.where(seen, 0.0, -1e30)
    factor = width ** (-0.5) * LOG2E
    for kv in range(kv_heads):
        key = kv_ref[:, kv * tokens : (kv + 1) * tokens, :].reshape(count, width)
        start = (kv_heads + kv) * tokens
        value = kv_ref[:, start : start + tokens, :].reshape(count, width)
        for group in range(head_groups):
            head = kv * head_groups + group
            scores = lax.dot_general(
                q_ref[head], key, (((1,), (1,)), ((), ())), preferred_element_type=F32
            )
            scores = scores + bias_ref[...]
            top = jnp.max(scores, axis=1, keepdims=True)
            weights = jnp.exp2((scores - top) * factor)
            total = jnp.sum(weights, axis=1, keepdims=True)
            mixed = jnp.dot(weights.astype(BF), value, preferred_element_type=F32)
            made_ref[head, :, :width] = jnp.broadcast_to(top, (tokens, width))
            made_ref[head, :, width : 2 * width] = jnp.broadcast_to(total, (tokens, width))
            made_ref[head, :, 2 * width :] = mixed


def merge_heads(first_ref, second_ref, head, width):
    factor = width ** (-0.5) * LOG2E
    parts = []
    for ref in (first_ref, second_ref):
        parts.append([ref[head, :, n * width : (n + 1) * width] for n in range(3)])
    top = jnp.maximum(parts[0][0], parts[1][0])
    keep = [jnp.exp2((part[0] - top) * factor) for part in parts]
    total = parts[0][1] * keep[0] + parts[1][1] * keep[1]
    mixed = parts[0][2] * keep[0] + parts[1][2] * keep[1]
    return top, total, mixed


def attend(carry, head_groups, q, kv, place, low, high):
    heads, tokens, width = q.shape
    count = kv.shape[0] * tokens
    wide = 3 * width
    first = carry is None

    def kernel(*refs):
        out_ref, bias_ref, made_ref, held_ref, sems, held_sem = refs[-6:]
        if not first:
            held_copy = pltpu.make_async_copy(refs[5], held_ref, held_sem)
            held_copy.start()
        attend_heads(head_groups, *refs[:5], bias_ref, made_ref)
        if not first:
            held_copy.wait()
            for head in range(heads):
                merged = merge_heads(held_ref, made_ref, head, width)
                for n in range(3):
                    made_ref[head, :, n * width : (n + 1) * width] = merged[n]
        copy = pltpu.make_async_copy(made_ref, out_ref, sems)
        copy.start()
        copy.wait()

    vmem, far = pl.BlockSpec(memory_space=pltpu.VMEM), pl.BlockSpec(memory_space=pltpu.HBM)
    carry_shape = (heads, tokens, wide)
    return pl.pallas_call(
        kernel,
        out_shape=jax.ShapeDtypeStruct(carry_shape, F32),
        in_specs=[vmem] * 5 + ([] if first else [far]),
        out_specs=far,
        scratch_shapes=[
            pltpu.VMEM((tokens, count), F32),
            pltpu.VMEM(carry_shape, F32),
            pltpu.VMEM((8, 128) if first else carry_shape, F32),
            pltpu.SemaphoreType.DMA,
            pltpu.SemaphoreType.DMA,
        ],
        compiler_params=pltpu.CompilerParams(vmem_limit_bytes=(18 << 20) + 5 * tokens * count * 4),
        cost_estimate=CHEAP,
    )(q, kv, place, low, high, *(() if first else (carry,)))


def attend_and_project(
    half, inputs, other_inputs, carry, head_groups, q, kv, place, low, high, weight
):
    heads, tokens, width = q.shape
    count = kv.shape[0] * tokens
    features = weight.shape[1]
    pieces = 4
    rows = weight.shape[0] // pieces

    def kernel(*refs):
        half_ref, refs = refs[0], refs[1:]
        carry_ref, weight_ref, in_ref, other_ref, out_ref, send_ref = refs[5:11]
        bias_ref, held, made_ref, weight_held, heads_ref, in_held, held_sem, weight_sems, in_sems = (
            refs[11:]
        )
        held_copy = pltpu.make_async_copy(carry_ref, held, held_sem)
        held_copy.start()
        in_copies = [
            pltpu.make_async_copy(ref, in_held.at[n], in_sems.at[n])
            for n, ref in enumerate((in_ref, other_ref))
        ]
        for copy in in_copies:
            copy.start()
        copies = []
        for n in range(pieces):
            at = pl.ds(n * rows, rows)
            copies.append(
                pltpu.make_async_copy(weight_ref.at[at], weight_held.at[at], weight_sems.at[n])
            )
            copies[n].start()
        attend_heads(head_groups, *refs[:5], bias_ref, made_ref)
        held_copy.wait()
        for head in range(heads):
            _, total, mixed = merge_heads(held, made_ref, head, width)
            heads_ref[:, head * width : (head + 1) * width] = (mixed / total).astype(BF)
        for copy in copies:
            copy.wait()
        step = 512
        for at in range(0, features, step):
            made = contract(heads_ref[...], weight_held[:, at : at + step], False)
            out_ref[:, at : at + step] = made
            send_ref[:, at : at + step] = made.astype(BF)
        own = in_ref.shape[1]
        for n, copy in enumerate(in_copies):
            copy.wait()
            side_of = half_ref[0] if n == 0 else 1 - half_ref[0]
            lanes = pl.ds(pl.multiple_of(side_of * own, own), own)
            out_ref[:, lanes] += in_held[n].astype(F32)

    vmem, far = pl.BlockSpec(memory_space=pltpu.VMEM), pl.BlockSpec(memory_space=pltpu.HBM)
    return pl.pallas_call(
        kernel,
        out_shape=[jax.ShapeDtypeStruct((tokens, features), kind) for kind in (F32, BF)],
        in_specs=[pl.BlockSpec(memory_space=pltpu.SMEM)] + [vmem] * 5 + [far] * 4,
        out_specs=[vmem, vmem],
        scratch_shapes=[
            pltpu.VMEM((tokens, count), F32),
            pltpu.VMEM(carry.shape, F32),
            pltpu.VMEM(carry.shape, F32),
            pltpu.VMEM(weight.shape, BF),
            pltpu.VMEM((tokens, heads * width), BF),
            pltpu.VMEM((2, *inputs.shape), BF),
            pltpu.SemaphoreType.DMA,
            pltpu.SemaphoreType.DMA((pieces,)),
            pltpu.SemaphoreType.DMA((2,)),
        ],
        compiler_params=pltpu.CompilerParams(vmem_limit_bytes=58 << 20),
        cost_estimate=CHEAP,
    )(half.reshape(1), q, kv, place, low, high, carry, weight, inputs, other_inputs)


def call(kernel, out_shape, *operands, head=None):
    size = sum(x.size * x.dtype.itemsize for x in jax.tree.leaves((operands, out_shape)))
    vmem = pl.BlockSpec(memory_space=pltpu.VMEM)
    in_specs = [vmem] * len(operands)
    if head is not None:
        in_specs = [pl.BlockSpec(memory_space=pltpu.SMEM)] + in_specs
        operands = (head.reshape(1), *operands)
    return pl.pallas_call(
        kernel,
        out_shape=out_shape,
        in_specs=in_specs,
        out_specs=jax.tree.map(lambda _: vmem, out_shape),
        compiler_params=pltpu.CompilerParams(vmem_limit_bytes=size + 6 * 1024 * 1024),
        cost_estimate=CHEAP,
    )(*operands)


def contract(rows, weight, flipped):
    dims = (((1,), (1 if flipped else 0,)), ((), ()))
    return lax.dot_general(rows, weight, dims, preferred_element_type=F32)


def flat(ref, expert=None):
    blocks, rows, width = ref.shape[-3:]
    return (ref[...] if expert is None else ref[expert]).reshape(blocks * rows, width)


def features_of(half, refs):
    count = refs[0].shape[1 if len(refs) == 2 else 2] // 2
    return pl.ds(pl.multiple_of(half * count, count), count)


def to_hidden(rows, refs, e, half):
    spot = features_of(half, refs)
    if len(refs) == 2:
        made = [contract(rows, ref[e, spot, :], False) for ref in refs]
        return jnp.concatenate(made, axis=1)
    return contract(rows, refs[0][e, :, spot], True)


def from_hidden(rows, refs, e, half):
    spot = features_of(half, refs)
    if len(refs) == 2:
        width = refs[0].shape[2]
        made = [
            contract(rows[:, n * width : (n + 1) * width], refs[n][e, spot, :], True)
            for n in range(2)
        ]
        return made[0] + made[1]
    return contract(rows, refs[0][e, :, spot], False)


def hidden_width(weights):
    return weights[0].shape[2] * 2 if len(weights) == 2 else weights[0].shape[1]


def dispatch(matrix, level, apart):
    count, side, rows, _ = matrix.shape
    width = level[0].shape[1]

    def kernel(matrix_ref, *refs):
        level_refs, outs = refs[:side], refs[side:]
        for e in range(count):
            out_ref = outs[e] if apart else outs[0].at[e]
            for a in range(side):
                out_ref[a] = contract(matrix_ref[e, a], level_refs[a][...], False).astype(BF)

    if apart:
        shapes = [jax.ShapeDtypeStruct((side, rows, width), BF)] * count
    else:
        shapes = [jax.ShapeDtypeStruct((count, side, rows, width), BF)]
    made = call(kernel, shapes, matrix, *level)
    return made if apart else made[0]


def normalize(head, made, arrived, gain):
    rows, width = made.shape[0], gain.shape[1]

    def kernel(head_ref, made_ref, arrived_ref, gain_ref, *outs):
        def stream_of(half):
            lanes = pl.ds(pl.multiple_of(half * width, width), width)
            return (made_ref[:, lanes] + arrived_ref[:, lanes].astype(F32)).astype(BF)

        stream = stream_of(head_ref[0])
        wide = stream.astype(F32)
        other = stream_of(1 - head_ref[0]).astype(F32)
        squares = jnp.sum(wide * wide + other * other, axis=1, keepdims=True)
        inverse = lax.rsqrt(squares / D + 1e-06)
        outs[0][...] = (wide * inverse * gain_ref[...].astype(F32)).astype(BF)
        outs[1][...] = stream
        outs[2][...] = inverse

    shapes = [
        jax.ShapeDtypeStruct((rows, width), BF),
        jax.ShapeDtypeStruct((rows, width), BF),
        jax.ShapeDtypeStruct((rows, 1), F32),
    ]
    return call(kernel, shapes, made, arrived, gain, head=head)


def half_hidden(head, own, other, weights):
    count = len(own)
    side, rows, _ = own[0].shape
    width = hidden_width(weights)

    def kernel(head_ref, *refs):
        own_refs, other_refs = refs[:count], refs[count : 2 * count]
        refs, outs = refs[2 * count : -2 * count], refs[-2 * count :]
        for e in range(count):
            mine = to_hidden(flat(own_refs[e]), refs, e, head_ref[0])
            outs[2 * e][...] = mine.reshape(side, rows, width)
            theirs = to_hidden(flat(other_refs[e]), refs, e, 1 - head_ref[0])
            outs[2 * e + 1][...] = theirs.reshape(side, rows, width)

    shape = jax.ShapeDtypeStruct((side, rows, width), F32)
    made = call(kernel, [shape] * (2 * count), *own, *other, *weights, head=head)
    return [made[2 * e : 2 * e + 2] for e in range(count)]


def sum_hidden(half, own_refs, other_refs, refs, out_ref, e, start):
    side, rows = out_ref.shape[0], out_ref.shape[2]
    for b in range(side):
        if start is not None and b == 0:
            out_ref[0] = start[0][...]
        else:
            made = to_hidden(flat(own_refs[b]), refs, e, half)
            out_ref[b] = made.reshape(side, rows, made.shape[1])
    for a in range(side):
        if start is not None and a == 0:
            made = flat(start[1])
        else:
            made = to_hidden(flat(other_refs[a]), refs, e, 1 - half)
        for b in range(side):
            out_ref[b, a] += made[b * rows : (b + 1) * rows]


def whole_hidden(head, own, other, weights):
    side = len(own)
    count, _, rows, _ = own[0].shape

    def kernel(head_ref, *refs):
        weight_refs, out_ref = refs[2 * side : -1], refs[-1]
        for e in range(count):
            own_refs = [ref.at[e] for ref in refs[:side]]
            other_refs = [ref.at[e] for ref in refs[side : 2 * side]]
            sum_hidden(
                head_ref[0], own_refs, other_refs, weight_refs, out_ref.at[e], e, None
            )

    shape = jax.ShapeDtypeStruct((count, side, side, rows, hidden_width(weights)), F32)
    return call(kernel, shape, *own, *other, *weights, head=head)


def column(ref, a):
    side, rows, width = ref.shape[1:]
    return ref[a].reshape(side * rows, width)


def send_column(head_ref, rows_ref, refs, outs, e, k):
    made = from_hidden(column(rows_ref, k), refs, e, 1 - head_ref[0])
    outs[k][...] = made.astype(BF).reshape(outs[k].shape)


def forward(head, e, own, other, start, weights, down):
    side = len(own) + 1
    _, rows, features = own[0].shape
    width = hidden_width(weights)
    half = width // 2

    def kernel(head_ref, *refs):
        refs = list(refs)
        own_refs = [None] + [refs.pop(0) for _ in range(side - 1)]
        other_refs = [None] + [refs.pop(0) for _ in range(side - 1)]
        begin = [refs.pop(0), refs.pop(0)]
        weight_refs = [refs.pop(0), refs.pop(0)]
        down_ref, hidden_ref, units_ref = refs[:3]
        sum_hidden(head_ref[0], own_refs, other_refs, weight_refs, hidden_ref, e, begin)
        for a in range(side):
            for b in range(side):
                gate = hidden_ref[b, a, :, :half]
                upper = hidden_ref[b, a, :, half:]
                silu = gate / (1.0 + jnp.exp(-gate))
                units_ref[a, b] = (silu * upper).astype(BF)
        for k in range(side - 1, -1, -1):
            send_column(head_ref, units_ref, [down_ref], refs[3:], e, k)

    shapes = [
        jax.ShapeDtypeStruct((side, side, rows, width), F32),
        jax.ShapeDtypeStruct((side, side, rows, half), BF),
    ] + [jax.ShapeDtypeStruct((side, rows, features), BF)] * side
    made = call(kernel, shapes, *own, *other, *start, *weights, down, head=head)
    return made[0], made[1], made[2:]


def backward(head, hidden, units_grad, weights):
    count = len(hidden)
    side, _, rows, width = hidden[0].shape
    half = width // 2
    features = weights[0].shape[1] // 2
    blocks = side

    def kernel(head_ref, *refs):
        hidden_refs, (grad_ref, gate_ref, up_ref) = refs[:count], refs[count : count + 3]
        outs = refs[count + 3 :]
        for e in range(count):
            both_ref, sends = outs[e], outs[count + e * blocks : count + (e + 1) * blocks]
            for a in range(side):
                for b in range(side):
                    gate = hidden_refs[e][b, a, :, :half]
                    upper = hidden_refs[e][b, a, :, half:]
                    grad = grad_ref[e, b, a]
                    sigmoid = 1.0 / (1.0 + jnp.exp(-gate))
                    slope = sigmoid * (1.0 + gate * (1.0 - sigmoid))
                    both_ref[a, b, :, :half] = (grad * upper * slope).astype(BF)
                    both_ref[a, b, :, half:] = (grad * (gate * sigmoid)).astype(BF)
            for k in range(side - 1, -1, -1):
                send_column(head_ref, both_ref, [gate_ref, up_ref], sends, e, k)

    shapes = [jax.ShapeDtypeStruct((side, side, rows, width), BF)] * count + [
        jax.ShapeDtypeStruct((side, rows, features), BF)
    ] * (count * blocks)
    made = call(kernel, shapes, *hidden, units_grad, *weights, head=head)
    sends = [made[count + e * blocks : count + (e + 1) * blocks] for e in range(count)]
    return made[:count], sends


def finish(head, rows, weights, arrived, k):
    count = len(rows)
    side, block, features = arrived[0].shape

    def kernel(head_ref, *refs):
        rows_refs, weight_refs = refs[:count], refs[count : -count - 1]
        arrived_refs, out_ref = refs[-count - 1 : -1], refs[-1]
        for e in range(count):
            mine = jnp.concatenate([rows_refs[e][a, k] for a in range(side)], axis=0)
            made = from_hidden(mine, weight_refs, e, head_ref[0])
            for a in range(side):
                added = arrived_refs[e][a].astype(F32)
                added = made[a * block : (a + 1) * block] + added
                out_ref[e, a] = added.astype(BF)

    shape = jax.ShapeDtypeStruct((count, side, block, features), BF)
    return call(kernel, shape, *rows, *weights, *arrived, head=head)


def weight_grad(head, units, own, other):
    side = len(own)
    count, _, rows, features = own[0].shape
    width = units[0].shape[3]

    def kernel(head_ref, *refs):
        units_refs, refs, out_ref = refs[:count], refs[count:-1], refs[-1]
        dims = (((0,), (0,)), ((), ()))
        spot = pl.multiple_of(head_ref[0] * features, features)
        away = pl.multiple_of((1 - head_ref[0]) * features, features)
        for e in range(count):
            by_own = [units_refs[e][a, b] for b in range(side) for a in range(side)]
            by_other = [units_refs[e][a, b] for a in range(side) for b in range(side)]
            for order, refs_of, lane in (
                (by_own, refs[:side], spot),
                (by_other, refs[side:], away),
            ):
                left = jnp.concatenate(order, axis=0)
                right = jnp.concatenate([flat(ref, e) for ref in refs_of], axis=0)
                made = lax.dot_general(left, right, dims, preferred_element_type=F32)
                out_ref[e, :, pl.ds(lane, features)] = made.astype(BF)

    shape = jax.ShapeDtypeStruct((count, width, 2 * features), BF)
    return call(kernel, shape, *units, *own, *other, head=head)


def local(
    inputs,
    queries,
    keys,
    values,
    lengths,
    out_weight,
    norm_gain,
    expert_ids,
    gate_codes,
    gate_weight,
    up_weight,
    down_weight,
    cotangent,
):
    devices = lax.axis_size("ctx")
    position = lax.axis_index("ctx")
    head = lax.axis_index("head")
    deep, side = grid_of(devices)
    plane = side * side

    def swap(rows):
        return swap_cores(rows, devices)

    def z_masks(k):
        return (k * plane, k * plane)

    def a_masks(k):
        return (k, k * side)

    def b_masks(k):
        return (k * side, k)

    def along(array, masks_of, count):
        return [array] + [exchange(array, devices, masks_of(k)) for k in range(1, count)]

    local_tokens, local_heads, head_width = queries.shape
    kv_heads = keys.shape[1]
    head_groups = local_heads // kv_heads
    half_width = inputs.shape[1]
    capacity = max(2, 5 * TOK_DEV * TOP // (4 * EXP_DEV * devices))
    tokens = deep * local_tokens
    block_rows = -(-deep * capacity // 16) * 16

    joint = (gate_weight, up_weight)

    packed = jnp.concatenate(
        [
            keys.transpose(1, 0, 2).reshape(kv_heads * local_tokens, head_width),
            values.transpose(1, 0, 2).reshape(kv_heads * local_tokens, head_width),
            expert_ids.T.astype(BF),
            gate_codes.T.astype(BF),
        ],
        axis=0,
    )
    pack_z = jnp.stack(along(packed, z_masks, deep))
    pack_a = jnp.stack(along(pack_z, a_masks, side))
    pack_b = along(pack_a, b_masks, side)
    chunks = devices

    order = jnp.arange(chunks, dtype=jnp.int32)
    z_part, a_part, b_part = order % deep, order // deep % side, order // (deep * side)
    shift = jnp.where(head == 0, a_part + b_part * side, a_part * side + b_part)
    sources = position ^ (z_part * plane + shift)

    def places_of(owner):
        within = jnp.arange(local_tokens, dtype=jnp.int32)
        half = local_tokens // 2
        owner = owner[..., None]
        return jnp.where(
            within < half, owner * half + within, (2 * devices - 1 - owner) * half + within - half
        )

    docs_in = lengths.shape[0]
    upto = jnp.arange(docs_in)[:, None] <= jnp.arange(docs_in)[None, :]
    ends = jnp.sum(jnp.where(upto, lengths[:, None], 0), axis=0)
    high = places_of(position[None])[0][:, None]
    low = jnp.max(jnp.where(high >= ends[None, :], ends[None, :], 0), axis=1, keepdims=True)
    key_places = places_of(sources).reshape(side, 1, side * deep * local_tokens)
    grouped = queries.transpose(1, 0, 2)
    carry = None
    for k in range(side - 1):
        part = pack_b[k].reshape(side * deep, *packed.shape)
        carry = attend(carry, head_groups, grouped, part, key_places[k], low, high)
    part = pack_b[-1].reshape(side * deep, *packed.shape)
    made, made_bf = attend_and_project(
        head,
        inputs,
        swap(inputs),
        carry,
        head_groups,
        grouped,
        part,
        key_places[-1],
        low,
        high,
        out_weight,
    )

    upstream = cotangent.astype(F32)
    cot_z = along(after(cotangent, pack_z), z_masks, deep)
    cot_z = jnp.stack(after(tuple(cot_z), made_bf)).reshape(tokens, half_width)
    cot_a = along(cot_z, a_masks, side)

    arrived = swap(made_bf)
    normed, stream, inverse = normalize(head, made, arrived, norm_gain.reshape(1, half_width))
    wide = stream.astype(F32)
    gain = norm_gain.astype(F32)

    near = pack_a[..., -2 * TOP :, :].astype(jnp.int32)
    near_ids, near_codes = near[..., :TOP, :], near[..., TOP:, :].astype(F32)
    near_total = jnp.sum(near_codes, axis=-2)
    owners = position ^ (jnp.arange(side, dtype=jnp.int32) * jnp.where(head == 0, side, 1))
    experts = owners[:, None] * EXP_DEV + jnp.arange(EXP_DEV, dtype=jnp.int32)
    hit = near_ids == experts[:, :, None, None, None, None]
    share = jnp.sum(jnp.where(hit, near_codes, 0.0), axis=-2) / near_total
    member = jnp.any(hit, axis=-2)
    before = jnp.arange(local_tokens)[:, None] < jnp.arange(local_tokens)[None, :]
    rank = jnp.einsum(
        "keazt,tu->keazu", member.astype(BF), before.astype(BF), preferred_element_type=F32
    ).astype(jnp.int32)
    slot = jnp.arange(deep, dtype=jnp.int32)[:, None] * capacity + rank
    slot = jnp.where(member, slot, -1)
    slot = slot.reshape(side, EXP_DEV, side, tokens)
    share = share.reshape(side, EXP_DEV, side, tokens)
    hot = slot[..., None, :] == jnp.arange(block_rows, dtype=jnp.int32)[:, None]
    hot_share = jnp.where(hot, share[..., None, :], 0.0).astype(BF)
    hot = hot.astype(BF)

    experts_here = range(EXP_DEV)

    def to_b(rows):
        return [exchange(rows[k], devices, b_masks(k)) for k in range(1, side)]

    def dense(matrix, got, a, lanes):
        out = 0.0
        for e in experts_here:
            for k in range(side):
                out = out + jnp.einsum(
                    "ru,rd->ud", matrix[k, e, a, :, lanes], got[e][k][a], preferred_element_type=F32
                )
        return out

    def return_pieces(matrix, got, step, waits):
        arrived, near_sum, across, passed = [], None, [], []
        for first in range(deep - step, -1, -step):
            lanes = slice(first * local_tokens, (first + step) * local_tokens)
            late = (waits, arrived[:1]) if first < deep - 2 * step else ()
            each = []
            for a in range(1, side):
                rows = after(dense(matrix, got, a, lanes).astype(BF), late)
                each.append(exchange(rows, devices, a_masks(a)))
            arrived += each
            level = dense(matrix, got, 0, lanes)
            for rows in after(tuple(each), level):
                level = level + rows.astype(F32)
            for z in range(first + step - 1, first - 1, -1):
                near_sum = level[(z - first) * local_tokens : (z - first + 1) * local_tokens]
                if z > 0:
                    passed.append(near_sum.astype(BF))
                    across.append(exchange(passed[-1], devices, z_masks(z)))
        return arrived, near_sum, across

    def last_sum(near_sum, across):
        for rows in across:
            near_sum = near_sum + rows.astype(F32)
        return near_sum

    norm_z = along(normed, z_masks, deep)
    cot_a = list(after(tuple(cot_a), normed))
    cot_out = [dispatch(hot_share[k], cot_a, False) for k in range(side)]
    incoming = [cot_out[0]] + to_b(cot_out)
    incoming_other = [swap(rows) for rows in incoming]
    norm_z = jnp.stack(after(tuple(norm_z), *cot_out)).reshape(tokens, half_width)
    norm_a = along(norm_z, a_masks, side)
    norm_out = [None] + [dispatch(hot[k], norm_a, False) for k in range(1, side)]
    norm_b = to_b(norm_out)
    norm_out[0] = dispatch(after(hot[0], norm_out[1:]), norm_a, True)
    units_grad = whole_hidden(head, incoming, incoming_other, (down_weight,))
    start = half_hidden(head, norm_out[0], [swap(rows) for rows in norm_out[0]], joint)
    norm_b = after(tuple(norm_b), (start, units_grad))

    hidden, units, theirs = [], [], []
    own_rows = [[rows[e] for rows in norm_b] for e in experts_here]
    other_rows = [[swap(rows) for rows in each] for each in own_rows]
    for e in experts_here:
        other = list(after(tuple(other_rows[e]), units))
        made = forward(head, e, own_rows[e], other, start[e], joint, down_weight)
        hidden.append(made[0])
        units.append(made[1])
        theirs.append(made[2])

    def finish_all(rows, weights, theirs):
        done = [None] * side
        for k in range(side - 1, -1, -1):
            arrived = [swap(each[k]) for each in theirs]
            done[k] = finish(head, rows, weights, arrived, k)
        return done

    total = finish_all(units, (down_weight,), theirs)
    sent = to_b(total)
    both, theirs = backward(head, list(after(tuple(hidden), total)), units_grad, joint)
    back_total = finish_all(both, joint, theirs)
    sent = after(tuple(sent), both)
    total = [total[0]] + list(sent)
    got = [[rows[e] for rows in total] for e in experts_here]
    arrived, near_sum, across = return_pieces(hot_share, got, 2, ())
    back_total = [back_total[0]] + to_b([None] + list(after(tuple(back_total[1:]), arrived[: side - 1])))
    got = [[rows[e] for rows in back_total] for e in experts_here]
    arrived, back_sum, back_across = return_pieces(hot, got, 2, across)
    output = (wide + last_sum(near_sum, across[::-1])).astype(BF)
    down_grad = weight_grad(head, after(tuple(units), arrived), incoming, incoming_other)
    scaled = last_sum(back_sum, after(tuple(back_across[::-1]), (down_grad, output))) * gain
    inner = jnp.sum(scaled * wide, axis=1, keepdims=True)
    inner = inner + swap(inner)
    input_grad = (upstream + inverse * scaled - wide * inverse**3 * inner / D).astype(BF)
    norm_term = (inverse**2 * inner / D**0.5)[:, 0]
    return (output, input_grad, down_grad, norm_term)


def solution(mesh):
    in_specs = (
        P("ctx", "head"),
        P("ctx", "head", None),
        P("ctx", "head", None),
        P("ctx", "head", None),
        P(),
        P("head", None),
        P("head"),
        P("ctx", None),
        P("ctx", None),
        P("ctx", None, "head"),
        P("ctx", None, "head"),
        P("ctx", "head", None),
        P("ctx", "head"),
    )
    out_specs = (P("ctx", "head"), P("ctx", "head"), P("ctx", "head", None), P("ctx"))
    return jax.shard_map(local, mesh=mesh, in_specs=in_specs, out_specs=out_specs, check_vma=False)
```

```python
import jax
import jax.numpy as jnp
from jax import lax
from jax.experimental import pallas as pl
from jax.experimental.pallas import tpu as pltpu
from jax.sharding import PartitionSpec as P

D = 2048
TOP = 8
EXP_DEV = 2
TOK_DEV = 128
BF = jnp.bfloat16
F32 = jnp.float32
AXES = ("ctx", "head")
CHEAP = pl.CostEstimate(flops=1, bytes_accessed=1, transcendentals=0)


def grid_of(devices):
    side = 2 if devices < 64 else 4
    return devices // (side * side), side


def exchange(array, devices, masks):
    pairs = [
        (c * 2 + h, (c ^ masks[h]) * 2 + h) for c in range(devices) for h in range(2)
    ]
    return lax.ppermute(array, AXES, pairs)


def swap_cores(array, devices):
    pairs = [(c * 2 + h, c * 2 + 1 - h) for c in range(devices) for h in range(2)]
    return lax.ppermute(array, AXES, pairs)


LOG2E = 1.4426950408889634


def after(value, *others):
    return lax.optimization_barrier((value, others))[0]


def attend_heads(head_groups, q_ref, kv_ref, place_ref, low_ref, high_ref, bias_ref, made_ref):
    heads, tokens, width = q_ref.shape
    chunks = kv_ref.shape[0]
    count = chunks * tokens
    kv_heads = heads // head_groups
    place = place_ref[...]
    seen = (place >= low_ref[...]) & (place <= high_ref[...])
    bias_ref[...] = jnp.where(seen, 0.0, -1e30)
    factor = width ** (-0.5) * LOG2E
    for kv in range(kv_heads):
        key = kv_ref[:, kv * tokens : (kv + 1) * tokens, :].reshape(count, width)
        start = (kv_heads + kv) * tokens
        value = kv_ref[:, start : start + tokens, :].reshape(count, width)
        for group in range(head_groups):
            head = kv * head_groups + group
            scores = lax.dot_general(
                q_ref[head], key, (((1,), (1,)), ((), ())), preferred_element_type=F32
            )
            scores = scores + bias_ref[...]
            top = jnp.max(scores, axis=1, keepdims=True)
            weights = jnp.exp2((scores - top) * factor)
            total = jnp.sum(weights, axis=1, keepdims=True)
            mixed = jnp.dot(weights.astype(BF), value, preferred_element_type=F32)
            made_ref[head, :, :width] = jnp.broadcast_to(top, (tokens, width))
            made_ref[head, :, width : 2 * width] = jnp.broadcast_to(total, (tokens, width))
            made_ref[head, :, 2 * width :] = mixed


def merge_heads(first_ref, second_ref, head, width):
    factor = width ** (-0.5) * LOG2E
    parts = []
    for ref in (first_ref, second_ref):
        parts.append([ref[head, :, n * width : (n + 1) * width] for n in range(3)])
    top = jnp.maximum(parts[0][0], parts[1][0])
    keep = [jnp.exp2((part[0] - top) * factor) for part in parts]
    total = parts[0][1] * keep[0] + parts[1][1] * keep[1]
    mixed = parts[0][2] * keep[0] + parts[1][2] * keep[1]
    return top, total, mixed


def attend(carry, head_groups, q, kv, place, low, high):
    heads, tokens, width = q.shape
    count = kv.shape[0] * tokens
    wide = 3 * width
    first = carry is None

    def kernel(*refs):
        out_ref, bias_ref, made_ref, held_ref, sems, held_sem = refs[-6:]
        if not first:
            held_copy = pltpu.make_async_copy(refs[5], held_ref, held_sem)
            held_copy.start()
        attend_heads(head_groups, *refs[:5], bias_ref, made_ref)
        if not first:
            held_copy.wait()
            for head in range(heads):
                merged = merge_heads(held_ref, made_ref, head, width)
                for n in range(3):
                    made_ref[head, :, n * width : (n + 1) * width] = merged[n]
        copy = pltpu.make_async_copy(made_ref, out_ref, sems)
        copy.start()
        copy.wait()

    vmem, far = pl.BlockSpec(memory_space=pltpu.VMEM), pl.BlockSpec(memory_space=pltpu.HBM)
    carry_shape = (heads, tokens, wide)
    return pl.pallas_call(
        kernel,
        out_shape=jax.ShapeDtypeStruct(carry_shape, F32),
        in_specs=[vmem] * 5 + ([] if first else [far]),
        out_specs=far,
        scratch_shapes=[
            pltpu.VMEM((tokens, count), F32),
            pltpu.VMEM(carry_shape, F32),
            pltpu.VMEM((8, 128) if first else carry_shape, F32),
            pltpu.SemaphoreType.DMA,
            pltpu.SemaphoreType.DMA,
        ],
        compiler_params=pltpu.CompilerParams(vmem_limit_bytes=(18 << 20) + 5 * tokens * count * 4),
        cost_estimate=CHEAP,
    )(q, kv, place, low, high, *(() if first else (carry,)))


def attend_and_project(
    half, inputs, other_inputs, carry, head_groups, q, kv, place, low, high, weight
):
    heads, tokens, width = q.shape
    count = kv.shape[0] * tokens
    features = weight.shape[1]
    pieces = 4
    rows = weight.shape[0] // pieces

    def kernel(*refs):
        half_ref, refs = refs[0], refs[1:]
        carry_ref, weight_ref, in_ref, other_ref, out_ref, send_ref = refs[5:11]
        bias_ref, held, made_ref, weight_held, heads_ref, in_held, held_sem, weight_sems, in_sems = (
            refs[11:]
        )
        held_copy = pltpu.make_async_copy(carry_ref, held, held_sem)
        held_copy.start()
        in_copies = [
            pltpu.make_async_copy(ref, in_held.at[n], in_sems.at[n])
            for n, ref in enumerate((in_ref, other_ref))
        ]
        for copy in in_copies:
            copy.start()
        copies = []
        for n in range(pieces):
            at = pl.ds(n * rows, rows)
            copies.append(
                pltpu.make_async_copy(weight_ref.at[at], weight_held.at[at], weight_sems.at[n])
            )
            copies[n].start()
        attend_heads(head_groups, *refs[:5], bias_ref, made_ref)
        held_copy.wait()
        for head in range(heads):
            _, total, mixed = merge_heads(held, made_ref, head, width)
            heads_ref[:, head * width : (head + 1) * width] = (mixed / total).astype(BF)
        for copy in copies:
            copy.wait()
        step = 512
        for at in range(0, features, step):
            made = contract(heads_ref[...], weight_held[:, at : at + step], False)
            out_ref[:, at : at + step] = made
            send_ref[:, at : at + step] = made.astype(BF)
        own = in_ref.shape[1]
        for n, copy in enumerate(in_copies):
            copy.wait()
            side_of = half_ref[0] if n == 0 else 1 - half_ref[0]
            lanes = pl.ds(pl.multiple_of(side_of * own, own), own)
            out_ref[:, lanes] += in_held[n].astype(F32)

    vmem, far = pl.BlockSpec(memory_space=pltpu.VMEM), pl.BlockSpec(memory_space=pltpu.HBM)
    return pl.pallas_call(
        kernel,
        out_shape=[jax.ShapeDtypeStruct((tokens, features), kind) for kind in (F32, BF)],
        in_specs=[pl.BlockSpec(memory_space=pltpu.SMEM)] + [vmem] * 5 + [far] * 4,
        out_specs=[vmem, vmem],
        scratch_shapes=[
            pltpu.VMEM((tokens, count), F32),
            pltpu.VMEM(carry.shape, F32),
            pltpu.VMEM(carry.shape, F32),
            pltpu.VMEM(weight.shape, BF),
            pltpu.VMEM((tokens, heads * width), BF),
            pltpu.VMEM((2, *inputs.shape), BF),
            pltpu.SemaphoreType.DMA,
            pltpu.SemaphoreType.DMA((pieces,)),
            pltpu.SemaphoreType.DMA((2,)),
        ],
        compiler_params=pltpu.CompilerParams(vmem_limit_bytes=58 << 20),
        cost_estimate=CHEAP,
    )(half.reshape(1), q, kv, place, low, high, carry, weight, inputs, other_inputs)


def call(kernel, out_shape, *operands, head=None):
    size = sum(x.size * x.dtype.itemsize for x in jax.tree.leaves((operands, out_shape)))
    vmem = pl.BlockSpec(memory_space=pltpu.VMEM)
    in_specs = [vmem] * len(operands)
    if head is not None:
        in_specs = [pl.BlockSpec(memory_space=pltpu.SMEM)] + in_specs
        operands = (head.reshape(1), *operands)
    return pl.pallas_call(
        kernel,
        out_shape=out_shape,
        in_specs=in_specs,
        out_specs=jax.tree.map(lambda _: vmem, out_shape),
        compiler_params=pltpu.CompilerParams(vmem_limit_bytes=size + 6 * 1024 * 1024),
        cost_estimate=CHEAP,
    )(*operands)


def contract(rows, weight, flipped):
    dims = (((1,), (1 if flipped else 0,)), ((), ()))
    return lax.dot_general(rows, weight, dims, preferred_element_type=F32)


def flat(ref, expert=None):
    blocks, rows, width = ref.shape[-3:]
    return (ref[...] if expert is None else ref[expert]).reshape(blocks * rows, width)


def features_of(half, refs):
    count = refs[0].shape[1 if len(refs) == 2 else 2] // 2
    return pl.ds(pl.multiple_of(half * count, count), count)


def to_hidden(rows, refs, e, half):
    spot = features_of(half, refs)
    if len(refs) == 2:
        made = [contract(rows, ref[e, spot, :], False) for ref in refs]
        return jnp.concatenate(made, axis=1)
    return contract(rows, refs[0][e, :, spot], True)


def from_hidden(rows, refs, e, half):
    spot = features_of(half, refs)
    if len(refs) == 2:
        width = refs[0].shape[2]
        made = [
            contract(rows[:, n * width : (n + 1) * width], refs[n][e, spot, :], True)
            for n in range(2)
        ]
        return made[0] + made[1]
    return contract(rows, refs[0][e, :, spot], False)


def hidden_width(weights):
    return weights[0].shape[2] * 2 if len(weights) == 2 else weights[0].shape[1]


def dispatch(matrix, level, apart):
    count, side, rows, _ = matrix.shape
    width = level[0].shape[1]

    def kernel(matrix_ref, *refs):
        level_refs, outs = refs[:side], refs[side:]
        for e in range(count):
            out_ref = outs[e] if apart else outs[0].at[e]
            for a in range(side):
                out_ref[a] = contract(matrix_ref[e, a], level_refs[a][...], False).astype(BF)

    if apart:
        shapes = [jax.ShapeDtypeStruct((side, rows, width), BF)] * count
    else:
        shapes = [jax.ShapeDtypeStruct((count, side, rows, width), BF)]
    made = call(kernel, shapes, matrix, *level)
    return made if apart else made[0]


def normalize(head, made, arrived, gain):
    rows, width = made.shape[0], gain.shape[1]

    def kernel(head_ref, made_ref, arrived_ref, gain_ref, *outs):
        def stream_of(half):
            lanes = pl.ds(pl.multiple_of(half * width, width), width)
            return (made_ref[:, lanes] + arrived_ref[:, lanes].astype(F32)).astype(BF)

        stream = stream_of(head_ref[0])
        wide = stream.astype(F32)
        other = stream_of(1 - head_ref[0]).astype(F32)
        squares = jnp.sum(wide * wide + other * other, axis=1, keepdims=True)
        inverse = lax.rsqrt(squares / D + 1e-06)
        outs[0][...] = (wide * inverse * gain_ref[...].astype(F32)).astype(BF)
        outs[1][...] = stream
        outs[2][...] = inverse

    shapes = [
        jax.ShapeDtypeStruct((rows, width), BF),
        jax.ShapeDtypeStruct((rows, width), BF),
        jax.ShapeDtypeStruct((rows, 1), F32),
    ]
    return call(kernel, shapes, made, arrived, gain, head=head)


def half_hidden(head, own, other, weights):
    count = len(own)
    side, rows, _ = own[0].shape
    width = hidden_width(weights)

    def kernel(head_ref, *refs):
        own_refs, other_refs = refs[:count], refs[count : 2 * count]
        refs, outs = refs[2 * count : -2 * count], refs[-2 * count :]
        for e in range(count):
            mine = to_hidden(flat(own_refs[e]), refs, e, head_ref[0])
            outs[2 * e][...] = mine.reshape(side, rows, width)
            theirs = to_hidden(flat(other_refs[e]), refs, e, 1 - head_ref[0])
            outs[2 * e + 1][...] = theirs.reshape(side, rows, width)

    shape = jax.ShapeDtypeStruct((side, rows, width), F32)
    made = call(kernel, [shape] * (2 * count), *own, *other, *weights, head=head)
    return [made[2 * e : 2 * e + 2] for e in range(count)]


def sum_hidden(half, own_refs, other_refs, refs, out_ref, e, start):
    side, rows = out_ref.shape[0], out_ref.shape[2]
    for b in range(side):
        if start is not None and b == 0:
            out_ref[0] = start[0][...]
        else:
            made = to_hidden(flat(own_refs[b]), refs, e, half)
            out_ref[b] = made.reshape(side, rows, made.shape[1])
    for a in range(side):
        if start is not None and a == 0:
            made = flat(start[1])
        else:
            made = to_hidden(flat(other_refs[a]), refs, e, 1 - half)
        for b in range(side):
            out_ref[b, a] += made[b * rows : (b + 1) * rows]


def whole_hidden(head, own, other, weights):
    side = len(own)
    count, _, rows, _ = own[0].shape

    def kernel(head_ref, *refs):
        weight_refs, out_ref = refs[2 * side : -1], refs[-1]
        for e in range(count):
            own_refs = [ref.at[e] for ref in refs[:side]]
            other_refs = [ref.at[e] for ref in refs[side : 2 * side]]
            sum_hidden(
                head_ref[0], own_refs, other_refs, weight_refs, out_ref.at[e], e, None
            )

    shape = jax.ShapeDtypeStruct((count, side, side, rows, hidden_width(weights)), F32)
    return call(kernel, shape, *own, *other, *weights, head=head)


def column(ref, a):
    side, rows, width = ref.shape[1:]
    return ref[a].reshape(side * rows, width)


def send_column(head_ref, rows_ref, refs, outs, e, k):
    made = from_hidden(column(rows_ref, k), refs, e, 1 - head_ref[0])
    outs[k][...] = made.astype(BF).reshape(outs[k].shape)


def forward(head, e, own, other, start, weights, down):
    side = len(own) + 1
    _, rows, features = own[0].shape
    width = hidden_width(weights)
    half = width // 2

    def kernel(head_ref, *refs):
        refs = list(refs)
        own_refs = [None] + [refs.pop(0) for _ in range(side - 1)]
        other_refs = [None] + [refs.pop(0) for _ in range(side - 1)]
        begin = [refs.pop(0), refs.pop(0)]
        weight_refs = [refs.pop(0), refs.pop(0)]
        down_ref, hidden_ref, units_ref = refs[:3]
        sum_hidden(head_ref[0], own_refs, other_refs, weight_refs, hidden_ref, e, begin)
        for a in range(side):
            for b in range(side):
                gate = hidden_ref[b, a, :, :half]
                upper = hidden_ref[b, a, :, half:]
                silu = gate / (1.0 + jnp.exp(-gate))
                units_ref[a, b] = (silu * upper).astype(BF)
        for k in range(side - 1, -1, -1):
            send_column(head_ref, units_ref, [down_ref], refs[3:], e, k)

    shapes = [
        jax.ShapeDtypeStruct((side, side, rows, width), F32),
        jax.ShapeDtypeStruct((side, side, rows, half), BF),
    ] + [jax.ShapeDtypeStruct((side, rows, features), BF)] * side
    made = call(kernel, shapes, *own, *other, *start, *weights, down, head=head)
    return made[0], made[1], made[2:]


def backward(head, hidden, units_grad, weights):
    count = len(hidden)
    side, _, rows, width = hidden[0].shape
    half = width // 2
    features = weights[0].shape[1] // 2
    blocks = side

    def kernel(head_ref, *refs):
        hidden_refs, (grad_ref, gate_ref, up_ref) = refs[:count], refs[count : count + 3]
        outs = refs[count + 3 :]
        for e in range(count):
            both_ref, sends = outs[e], outs[count + e * blocks : count + (e + 1) * blocks]
            for a in range(side):
                for b in range(side):
                    gate = hidden_refs[e][b, a, :, :half]
                    upper = hidden_refs[e][b, a, :, half:]
                    grad = grad_ref[e, b, a]
                    sigmoid = 1.0 / (1.0 + jnp.exp(-gate))
                    slope = sigmoid * (1.0 + gate * (1.0 - sigmoid))
                    both_ref[a, b, :, :half] = (grad * upper * slope).astype(BF)
                    both_ref[a, b, :, half:] = (grad * (gate * sigmoid)).astype(BF)
            for k in range(side - 1, -1, -1):
                send_column(head_ref, both_ref, [gate_ref, up_ref], sends, e, k)

    shapes = [jax.ShapeDtypeStruct((side, side, rows, width), BF)] * count + [
        jax.ShapeDtypeStruct((side, rows, features), BF)
    ] * (count * blocks)
    made = call(kernel, shapes, *hidden, units_grad, *weights, head=head)
    sends = [made[count + e * blocks : count + (e + 1) * blocks] for e in range(count)]
    return made[:count], sends


def finish(head, rows, weights, arrived, k):
    count = len(rows)
    side, block, features = arrived[0].shape

    def kernel(head_ref, *refs):
        rows_refs, weight_refs = refs[:count], refs[count : -count - 1]
        arrived_refs, out_ref = refs[-count - 1 : -1], refs[-1]
        for e in range(count):
            mine = jnp.concatenate([rows_refs[e][a, k] for a in range(side)], axis=0)
            made = from_hidden(mine, weight_refs, e, head_ref[0])
            for a in range(side):
                added = arrived_refs[e][a].astype(F32)
                added = made[a * block : (a + 1) * block] + added
                out_ref[e, a] = added.astype(BF)

    shape = jax.ShapeDtypeStruct((count, side, block, features), BF)
    return call(kernel, shape, *rows, *weights, *arrived, head=head)


def weight_grad(head, units, own, other):
    side = len(own)
    count, _, rows, features = own[0].shape
    width = units[0].shape[3]

    def kernel(head_ref, *refs):
        units_refs, refs, out_ref = refs[:count], refs[count:-1], refs[-1]
        dims = (((0,), (0,)), ((), ()))
        spot = pl.multiple_of(head_ref[0] * features, features)
        away = pl.multiple_of((1 - head_ref[0]) * features, features)
        for e in range(count):
            by_own = [units_refs[e][a, b] for b in range(side) for a in range(side)]
            by_other = [units_refs[e][a, b] for a in range(side) for b in range(side)]
            for order, refs_of, lane in (
                (by_own, refs[:side], spot),
                (by_other, refs[side:], away),
            ):
                left = jnp.concatenate(order, axis=0)
                right = jnp.concatenate([flat(ref, e) for ref in refs_of], axis=0)
                made = lax.dot_general(left, right, dims, preferred_element_type=F32)
                out_ref[e, :, pl.ds(lane, features)] = made.astype(BF)

    shape = jax.ShapeDtypeStruct((count, width, 2 * features), BF)
    return call(kernel, shape, *units, *own, *other, head=head)


def local(
    inputs,
    queries,
    keys,
    values,
    lengths,
    out_weight,
    norm_gain,
    expert_ids,
    gate_codes,
    gate_weight,
    up_weight,
    down_weight,
    cotangent,
):
    devices = lax.axis_size("ctx")
    position = lax.axis_index("ctx")
    head = lax.axis_index("head")
    deep, side = grid_of(devices)
    plane = side * side

    def swap(rows):
        return swap_cores(rows, devices)

    def z_masks(k):
        return (k * plane, k * plane)

    def a_masks(k):
        return (k, k * side)

    def b_masks(k):
        return (k * side, k)

    def along(array, masks_of, count):
        return [array] + [exchange(array, devices, masks_of(k)) for k in range(1, count)]

    local_tokens, local_heads, head_width = queries.shape
    kv_heads = keys.shape[1]
    head_groups = local_heads // kv_heads
    half_width = inputs.shape[1]
    capacity = max(2, 5 * TOK_DEV * TOP // (4 * EXP_DEV * devices))
    tokens = deep * local_tokens
    block_rows = -(-deep * capacity // 16) * 16

    joint = (gate_weight, up_weight)

    packed = jnp.concatenate(
        [
            keys.transpose(1, 0, 2).reshape(kv_heads * local_tokens, head_width),
            values.transpose(1, 0, 2).reshape(kv_heads * local_tokens, head_width),
            expert_ids.T.astype(BF),
            gate_codes.T.astype(BF),
        ],
        axis=0,
    )
    pack_z = jnp.stack(along(packed, z_masks, deep))
    pack_a = jnp.stack(along(pack_z, a_masks, side))
    pack_b = along(pack_a, b_masks, side)
    chunks = devices

    order = jnp.arange(chunks, dtype=jnp.int32)
    z_part, a_part, b_part = order % deep, order // deep % side, order // (deep * side)
    shift = jnp.where(head == 0, a_part + b_part * side, a_part * side + b_part)
    sources = position ^ (z_part * plane + shift)

    def places_of(owner):
        within = jnp.arange(local_tokens, dtype=jnp.int32)
        half = local_tokens // 2
        owner = owner[..., None]
        return jnp.where(
            within < half, owner * half + within, (2 * devices - 1 - owner) * half + within - half
        )

    docs_in = lengths.shape[0]
    upto = jnp.arange(docs_in)[:, None] <= jnp.arange(docs_in)[None, :]
    ends = jnp.sum(jnp.where(upto, lengths[:, None], 0), axis=0)
    high = places_of(position[None])[0][:, None]
    low = jnp.max(jnp.where(high >= ends[None, :], ends[None, :], 0), axis=1, keepdims=True)
    key_places = places_of(sources).reshape(side, 1, side * deep * local_tokens)
    grouped = queries.transpose(1, 0, 2)
    carry = None
    for k in range(side - 1):
        part = pack_b[k].reshape(side * deep, *packed.shape)
        carry = attend(carry, head_groups, grouped, part, key_places[k], low, high)
    part = pack_b[-1].reshape(side * deep, *packed.shape)
    made, made_bf = attend_and_project(
        head,
        inputs,
        swap(inputs),
        carry,
        head_groups,
        grouped,
        part,
        key_places[-1],
        low,
        high,
        out_weight,
    )

    upstream = cotangent.astype(F32)
    cot_z = along(after(cotangent, pack_z), z_masks, deep)
    cot_z = jnp.stack(after(tuple(cot_z), made_bf)).reshape(tokens, half_width)
    cot_a = along(cot_z, a_masks, side)

    arrived = swap(made_bf)
    normed, stream, inverse = normalize(head, made, arrived, norm_gain.reshape(1, half_width))
    wide = stream.astype(F32)
    gain = norm_gain.astype(F32)

    near = pack_a[..., -2 * TOP :, :].astype(jnp.int32)
    near_ids, near_codes = near[..., :TOP, :], near[..., TOP:, :].astype(F32)
    near_total = jnp.sum(near_codes, axis=-2)
    owners = position ^ (jnp.arange(side, dtype=jnp.int32) * jnp.where(head == 0, side, 1))
    experts = owners[:, None] * EXP_DEV + jnp.arange(EXP_DEV, dtype=jnp.int32)
    hit = near_ids == experts[:, :, None, None, None, None]
    share = jnp.sum(jnp.where(hit, near_codes, 0.0), axis=-2) / near_total
    member = jnp.any(hit, axis=-2)
    before = jnp.arange(local_tokens)[:, None] < jnp.arange(local_tokens)[None, :]
    rank = jnp.einsum(
        "keazt,tu->keazu", member.astype(BF), before.astype(BF), preferred_element_type=F32
    ).astype(jnp.int32)
    slot = jnp.arange(deep, dtype=jnp.int32)[:, None] * capacity + rank
    slot = jnp.where(member, slot, -1)
    slot = slot.reshape(side, EXP_DEV, side, tokens)
    share = share.reshape(side, EXP_DEV, side, tokens)
    hot = slot[..., None, :] == jnp.arange(block_rows, dtype=jnp.int32)[:, None]
    hot_share = jnp.where(hot, share[..., None, :], 0.0).astype(BF)
    hot = hot.astype(BF)

    experts_here = range(EXP_DEV)

    def to_b(rows):
        return [exchange(rows[k], devices, b_masks(k)) for k in range(1, side)]

    def dense(matrix, got, a, lanes):
        out = 0.0
        for k in range(side):
            out = out + jnp.einsum(
                "eru,erd->ud",
                matrix[k, :, a, :, lanes],
                got[k][:, a],
                preferred_element_type=F32,
            )
        return out

    def return_pieces(matrix, got, step, waits):
        arrived, near_sum, across, passed = [], None, [], []
        for first in range(deep - step, -1, -step):
            lanes = slice(first * local_tokens, (first + step) * local_tokens)
            late = (waits, arrived[:1]) if first < deep - 2 * step else ()
            each = []
            for a in range(1, side):
                rows = after(dense(matrix, got, a, lanes).astype(BF), late)
                each.append(exchange(rows, devices, a_masks(a)))
            arrived += each
            level = dense(matrix, got, 0, lanes)
            for rows in after(tuple(each), level):
                level = level + rows.astype(F32)
            for z in range(first + step - 1, first - 1, -1):
                near_sum = level[(z - first) * local_tokens : (z - first + 1) * local_tokens]
                if z > 0:
                    passed.append(near_sum.astype(BF))
                    across.append(exchange(passed[-1], devices, z_masks(z)))
        return arrived, near_sum, across

    def last_sum(near_sum, across):
        for rows in across:
            near_sum = near_sum + rows.astype(F32)
        return near_sum

    norm_z = along(normed, z_masks, deep)
    cot_a = list(after(tuple(cot_a), normed))
    cot_out = [dispatch(hot_share[k], cot_a, False) for k in range(side)]
    incoming = [cot_out[0]] + to_b(cot_out)
    incoming_other = [swap(rows) for rows in incoming]
    norm_z = jnp.stack(after(tuple(norm_z), *cot_out)).reshape(tokens, half_width)
    norm_a = along(norm_z, a_masks, side)
    norm_out = [None] + [dispatch(hot[k], norm_a, False) for k in range(1, side)]
    norm_b = to_b(norm_out)
    norm_out[0] = dispatch(after(hot[0], norm_out[1:]), norm_a, True)
    units_grad = whole_hidden(head, incoming, incoming_other, (down_weight,))
    start = half_hidden(head, norm_out[0], [swap(rows) for rows in norm_out[0]], joint)
    norm_b = after(tuple(norm_b), (start, units_grad))

    hidden, units, theirs = [], [], []
    own_rows = [[rows[e] for rows in norm_b] for e in experts_here]
    other_rows = [[swap(rows) for rows in each] for each in own_rows]
    for e in experts_here:
        other = list(after(tuple(other_rows[e]), units))
        made = forward(head, e, own_rows[e], other, start[e], joint, down_weight)
        hidden.append(made[0])
        units.append(made[1])
        theirs.append(made[2])

    def finish_all(rows, weights, theirs):
        done = [None] * side
        for k in range(side - 1, -1, -1):
            arrived = [swap(each[k]) for each in theirs]
            done[k] = finish(head, rows, weights, arrived, k)
        return done

    total = finish_all(units, (down_weight,), theirs)
    sent = to_b(total)
    both, theirs = backward(head, list(after(tuple(hidden), total)), units_grad, joint)
    back_total = finish_all(both, joint, theirs)
    sent = after(tuple(sent), back_total)
    total = [total[0]] + list(sent)
    got = total
    arrived, near_sum, across = return_pieces(hot_share, got, deep, ())
    back_total = [back_total[0]] + to_b([None] + list(after(tuple(back_total[1:]), arrived)))
    got = back_total
    arrived, back_sum, back_across = return_pieces(hot, got, 2, across)
    output = (wide + last_sum(near_sum, across)).astype(BF)
    down_grad = weight_grad(head, after(tuple(units), arrived), incoming, incoming_other)
    scaled = last_sum(back_sum, after(tuple(back_across[::-1]), (down_grad, output))) * gain
    inner = jnp.sum(scaled * wide, axis=1, keepdims=True)
    inner = inner + swap(inner)
    input_grad = (upstream + inverse * scaled - wide * inverse**3 * inner / D).astype(BF)
    norm_term = (inverse**2 * inner / D**0.5)[:, 0]
    return (output, input_grad, down_grad, norm_term)


def solution(mesh):
    in_specs = (
        P("ctx", "head"),
        P("ctx", "head", None),
        P("ctx", "head", None),
        P("ctx", "head", None),
        P(),
        P("head", None),
        P("head"),
        P("ctx", None),
        P("ctx", None),
        P("ctx", None, "head"),
        P("ctx", None, "head"),
        P("ctx", "head", None),
        P("ctx", "head"),
    )
    out_specs = (P("ctx", "head"), P("ctx", "head"), P("ctx", "head", None), P("ctx"))
    return jax.shard_map(local, mesh=mesh, in_specs=in_specs, out_specs=out_specs, check_vma=False)
```
